128 devices in a mesh: rows: 16 (over y, x), pb: 8 (over z, core).
Axes of the slice: x: 4, y: 4, z: 4, core: 2. Of those that a mesh axis runs over, the one named last changes fastest.
Arguments:
- lower_panel: bfloat16 [2, 16384, 2048], P(None, 'rows'), may hold values from -0.1875 to 0.1875
- sparse_desc: bfloat16 [2, 16384, 1024], P(None, 'rows', 'pb'), may hold values from -6 to 6
- query_desc: bfloat16 [8192, 1024], P('pb', 'rows'), may hold values from -6 to 6
- diag_inv: bfloat16 [2, 1024, 1024], replicated, may hold values from -0.1875 to 0.1875
Outputs:
- partial_solve: bfloat16 [2, 16384, 8192], P(None, 'rows', 'pb')
The draws below stay inside these ranges and needn't reach their ends.
All inputs are finite; a program needn't handle non-finite values.
Results may differ from the reference program's by a relative error of at most 0.006.
Values may be sent and summed in bfloat16 or wider, within the bound.
No kernel may reach another device: no remote copies, remote signals or barrier semaphores. Data moves between devices by JAX's collectives and lax.ppermute only.
A program may use at most 128 MiB of HBM per device.

```python
import jax
import jax.numpy as jnp

B = 1024
F = 1024
RB_DEV = 2
Q = 8192
N_ROWS = 16


def levels(key, extent, pieces, least, largest):
    def one(axis_at, blocks):
        steps = jax.random.uniform(jax.random.fold_in(jax.random.fold_in(key, 6), axis_at), (blocks,), jnp.float32, least / len(pieces), largest / len(pieces))
        return jnp.repeat(jnp.exp(steps), extent[axis_at] // blocks).reshape((-1,) + (1,) * (len(extent) - axis_at - 1))

    factor_of = one(*pieces[0])
    for cut in pieces[1:]:
        factor_of = factor_of * one(*cut)
    return factor_of


def bell_draw(key, shape, scale, reach, shards=(), kind=jnp.bfloat16):
    result = jax.random.normal(key, shape, jnp.float32) * scale
    if len(shards) > 0:
        result = levels(key, shape, shards, -0.22, 0.18) * result
    return jnp.clip(result, min=-reach, max=reach).astype(kind)


def setup_inputs(seed: int = 0) -> dict:
    key_list = jax.random.split(jax.random.key(seed), 5)
    return {
        "lower_panel": bell_draw(key_list[0], (RB_DEV, N_ROWS * B, 2 * B), B ** -0.5, 0.1875, ((1, 16),)),
        "sparse_desc": bell_draw(key_list[1], (RB_DEV, N_ROWS * B, F), 1.0, 6.0, ((1, 16), (2, 8))),
        "query_desc": bell_draw(key_list[2], (Q, F), 1.0, 6.0, ((0, 8), (1, 16))),
        "diag_inv": bell_draw(key_list[3], (2, B, B), B ** -0.5, 0.1875),
    }


def reference(lower_panel, sparse_desc, query_desc, diag_inv):
    width = diag_inv.shape[1]
    feats = query_desc.shape[1]
    dots = jnp.einsum('smf,qf->smq', sparse_desc.astype(jnp.float32), query_desc.astype(jnp.float32))
    scaled = dots / jnp.sqrt(jnp.float32(feats))
    kstar = scaled * scaled
    solved0 = jnp.dot(diag_inv[0], kstar[0, :width].astype(jnp.bfloat16), preferred_element_type=jnp.float32).astype(jnp.bfloat16)
    resid = kstar - jnp.einsum('smk,kq->smq', lower_panel[:, :, :width].astype(jnp.float32), solved0.astype(jnp.float32))
    solved1 = jnp.dot(diag_inv[1], resid[0, width:2 * width].astype(jnp.bfloat16), preferred_element_type=jnp.float32).astype(jnp.bfloat16)
    resid = resid - jnp.einsum('smk,kq->smq', lower_panel[:, :, width:].astype(jnp.float32), solved1.astype(jnp.float32))
    output = resid.astype(jnp.bfloat16)
    output = output.at[0, :width].set(solved0)
    output = output.at[0, width:2 * width].set(solved1)
    return output
```

```python
import jax
import jax.numpy as jnp
from jax import lax
from jax.experimental import pallas as pl
from jax.experimental.pallas import tpu as pltpu
from jax.sharding import PartitionSpec as P

BF16, F32 = jnp.bfloat16, jnp.float32
VMEM_BYTES = 56 * 1024 * 1024
N = 4
TILE = 256


def x_perm(d):
    return [(r, (r // N) * N + (r % N + d) % N) for r in range(N * N)]


def y_perm(d):
    return [(r, ((r // N + d) % N) * N + r % N) for r in range(N * N)]


def z_perm(d):
    return [(p, ((p // 2 + d) % N) * 2 + p % 2) for p in range(2 * N)]


SWAP = [(p, p ^ 1) for p in range(2 * N)]


def pick(index, choices):
    out = choices[0]
    for i in range(1, len(choices)):
        out = jnp.where(index == i, choices[i], out)
    return out


def after(value, *others):
    return lax.optimization_barrier((value,) + others)[0]


def params(**kw):
    return pltpu.CompilerParams(vmem_limit_bytes=VMEM_BYTES, **kw)


def cost(flops, moved):
    return pl.CostEstimate(flops=int(flops), bytes_accessed=int(moved), transcendentals=0)


def whole():
    return pl.BlockSpec(memory_space=pltpu.VMEM)


def place_features(at, refs, dst, rows=None):
    z, core = at[2], at[3]
    for i, ref in enumerate(refs):
        zz = lax.rem(z + (0, 3, 1, 2)[i % 4], 4)
        cc = core if i < 4 else 1 - core
        off = pl.multiple_of((zz * 2 + cc) * 128, 128)
        dst[:, pl.ds(off, 128)] = ref[...]


def kernel_slices(at, qt, s0, s1, s2, s3, s4, s5, s6, s7, k0, k1, feats):
    place_features(at, (s0, s1, s2, s3, s4, s5, s6, s7), feats)
    half = k0.shape[0]
    scale = 1.0 / (qt.shape[0] ** 0.5)

    def step(i, _):
        cols = pl.ds(pl.multiple_of(i * TILE, TILE), TILE)
        dots = jnp.dot(feats[...], qt[:, cols], preferred_element_type=F32) * scale
        k = dots * dots
        k0[:, cols] = k[:half].astype(BF16)
        k1[:, cols] = k[half:]
        return 0

    lax.fori_loop(0, qt.shape[1] // TILE, step, 0)


def place_rows(at, refs, dst):
    color = lax.rem(at[0] + 2 * at[1], 4)
    for add, ref in zip((0, 1, 3, 2), refs):
        off = pl.multiple_of(lax.rem(color + add, 4) * ref.shape[0], ref.shape[0])
        dst[pl.ds(off, ref.shape[0]), :] = ref[...]


def first_solve(at, a, b, c, d, inv, la, lb, k1, s0, t, rhs):
    place_rows(at, (a, b, c, d), rhs)
    core = at[3]
    half = la.shape[1]
    off_a = pl.multiple_of(core * half, half)
    off_b = pl.multiple_of((1 - core) * half, half)

    def step(i, _):
        cols = pl.ds(pl.multiple_of(i * TILE, TILE), TILE)
        s0[:, cols] = jnp.dot(inv[...], rhs[:, cols], preferred_element_type=F32).astype(BF16)
        low = jnp.dot(la[...], s0[pl.ds(off_a, half), cols], preferred_element_type=F32)
        low = low + jnp.dot(lb[...], s0[pl.ds(off_b, half), cols], preferred_element_type=F32)
        t[:, cols] = (k1[:, cols] - low).astype(BF16)
        return 0

    lax.fori_loop(0, rhs.shape[1] // TILE, step, 0)


def residual(at, qt, s0, low, p0, p1, p2, p3, p4, p5, p6, p7, out, feats):
    place_features(at, (p0, p1, p2, p3, p4, p5, p6, p7), feats)
    scale = 1.0 / (qt.shape[0] ** 0.5)
    dots = jnp.dot(feats[...], qt[...], preferred_element_type=F32) * scale
    out[...] = dots * dots - jnp.dot(low[...], s0[...], preferred_element_type=F32)


def last_step(at, a, b, c, d, inv, s0, low, res, out, rhs, s1):
    i = pl.program_id(0)
    here = at[0] + 4 * at[1]
    bm = out.shape[0]
    per_block = s1.shape[0] // bm

    @pl.when(i == 0)
    def _():
        place_rows(at, (a, b, c, d), rhs)

        def step(j, _):
            cols = pl.ds(pl.multiple_of(j * TILE, TILE), TILE)
            s1[:, cols] = jnp.dot(inv[...], rhs[:, cols], preferred_element_type=F32).astype(BF16)
            return 0

        lax.fori_loop(0, rhs.shape[1] // TILE, step, 0)

    rows = pl.ds(pl.multiple_of(lax.rem(i, per_block) * bm, bm), bm)
    first = i < per_block

    @pl.when(jnp.logical_and(first, here == 0))
    def _():
        out[...] = s0[rows, :]

    @pl.when(jnp.logical_and(first, here == 1))
    def _():
        out[...] = s1[rows, :]

    @pl.when(jnp.logical_not(jnp.logical_and(first, here < 2)))
    def _():
        out[...] = (res[...] - jnp.dot(low[...], s1[...], preferred_element_type=F32)).astype(BF16)


def per_device(lower_panel, sparse_desc, query_desc, diag_inv):
    blocks, width, _ = lower_panel.shape
    queries = query_desc.shape[0]
    here, part = lax.axis_index("rows"), lax.axis_index("pb")
    x, y = here % N, here // N
    z, core = part // 2, part % 2
    at = jnp.stack([x, y, z, core]).astype(jnp.int32)
    smem = pl.BlockSpec(memory_space=pltpu.SMEM)
    quarter = width // 4
    piece = sparse_desc.shape[2]
    feats = piece * 2 * N

    qt = query_desc.T
    qt = jnp.broadcast_to(qt[None], (N * N,) + qt.shape)
    qt = lax.all_to_all(qt, "rows", 0, 0, tiled=True).reshape(feats, queries)

    first = sparse_desc[0].reshape(4, quarter, piece)

    def two(d):
        return jnp.concatenate(
            [lax.dynamic_index_in_dim(first, (x + d + e) % 4, 0, False) for e in (0, 2)]
        )

    got = [two(0)] + [
        lax.ppermute(two(d), "rows", [(0, d), (1, (1 + d) % N)]) for d in (1, 2, 3)
    ]
    from0 = pick(x, got)
    from1 = pick((x + 3) % N, got)
    even = jnp.concatenate([from0[:quarter], from1[:quarter]])
    odd = jnp.concatenate([from0[quarter:], from1[quarter:]])
    got_y = [even] + [
        lax.ppermute(even if d == 2 else odd, "rows", [(c, d * N + c) for c in range(N)])
        for d in (1, 2, 3)
    ]
    mine = pick(y, got_y)
    slices = [mine] + [lax.ppermute(mine, "pb", z_perm(d)) for d in (1, -1, 2)]
    slices = slices + [lax.ppermute(v, "pb", SWAP) for v in slices]

    low = lax.dynamic_slice_in_dim(lower_panel[0], core * (width // 2), width // 2, 1)
    low = low.reshape(4, quarter, width // 2)
    low = after(low, got[1], got[2], got[3])

    def two_low(d):
        return jnp.concatenate([low[(1 + d) % 4], low[(3 + d) % 4]])

    got_l = [two_low(0)] + [
        lax.ppermute(two_low(d), "rows", [(1, (1 + d) % N)]) for d in (1, 2, 3)
    ]
    from_l = pick((x + 3) % N, got_l)
    even_l, odd_l = from_l[:quarter], from_l[quarter:]
    got_ly = [even_l] + [
        lax.ppermute(even_l if d == 2 else odd_l, "rows", [(c, d * N + c) for c in range(N)])
        for d in (1, 2, 3)
    ]
    low_a = pick(y, got_ly)
    low_b = lax.ppermute(low_a, "pb", SWAP)

    own = sparse_desc.reshape(blocks * width, piece)
    own_z = after(own, slices[1], slices[2], slices[3])
    envs = [own] + [lax.ppermute(own_z, "pb", z_perm(d)) for d in (1, -1, 2)]
    envs = envs + [lax.ppermute(v, "pb", SWAP) for v in envs]

    unit = 2 * width * feats * queries
    k0, k1 = pl.pallas_call(
        kernel_slices,
        out_shape=(
            jax.ShapeDtypeStruct((quarter, queries), BF16),
            jax.ShapeDtypeStruct((quarter, queries), F32),
        ),
        in_specs=[smem] + [whole()] * 9,
        out_specs=(whole(), whole()),
        scratch_shapes=[pltpu.VMEM((2 * quarter, feats), BF16)],
        compiler_params=params(),
        cost_estimate=cost(unit / 2, 5e6),
    )(at, qt, *slices)

    def neighbours(v):
        return (
            v,
            lax.ppermute(v, "rows", x_perm(-1)),
            lax.ppermute(v, "rows", x_perm(1)),
            lax.ppermute(v, "rows", y_perm(-1)),
        )

    block = pl.BlockSpec((None, width, width), lambda *_: (0, 0, 0), memory_space=pltpu.VMEM)
    s0, t = pl.pallas_call(
        first_solve,
        grid=(1,),
        out_shape=(
            jax.ShapeDtypeStruct((width, queries), BF16),
            jax.ShapeDtypeStruct((quarter, queries), BF16),
        ),
        in_specs=[smem] + [whole()] * 4 + [block] + [whole()] * 3,
        out_specs=(whole(), whole()),
        scratch_shapes=[pltpu.VMEM((width, queries), BF16)],
        compiler_params=params(),
        cost_estimate=cost(unit * 1.25, 8e6),
    )(at, *neighbours(k0), diag_inv, low_a, low_b, k1)

    bm = TILE
    rows = blocks * width
    panel = lower_panel.reshape(rows, 2 * width)
    res = pl.pallas_call(
        residual,
        grid=(rows // bm,),
        out_shape=jax.ShapeDtypeStruct((rows, queries), F32),
        in_specs=[smem, whole(), whole(), pl.BlockSpec((bm, width), lambda i: (i, 0))]
        + [pl.BlockSpec((bm, piece), lambda i: (i, 0))] * 8,
        out_specs=pl.BlockSpec((bm, queries), lambda i: (i, 0)),
        scratch_shapes=[pltpu.VMEM((bm, feats), BF16)],
        compiler_params=params(),
        cost_estimate=cost(unit * 4, 22e6),
    )(at, qt, s0, panel, *envs)

    block1 = pl.BlockSpec((None, width, width), lambda *_: (1, 0, 0), memory_space=pltpu.VMEM)
    out = pl.pallas_call(
        last_step,
        grid=(rows // bm,),
        out_shape=jax.ShapeDtypeStruct((rows, queries), BF16),
        in_specs=[smem]
        + [whole()] * 4
        + [
            block1,
            whole(),
            pl.BlockSpec((bm, width), lambda i: (i, 1)),
            pl.BlockSpec((bm, queries), lambda i: (i, 0)),
        ],
        out_specs=pl.BlockSpec((bm, queries), lambda i: (i, 0)),
        scratch_shapes=[pltpu.VMEM((width, queries), BF16), pltpu.VMEM((width, queries), BF16)],
        compiler_params=params(),
        cost_estimate=cost(unit * 3, 20e6),
    )(at, *neighbours(t), diag_inv, s0, panel, res)
    return out.reshape(blocks, width, queries)


def solution(mesh):
    return jax.shard_map(
        per_device,
        mesh=mesh,
        in_specs=(P(None, "rows", None), P(None, "rows", "pb"), P("pb", "rows"), P()),
        out_specs=P(None, "rows", "pb"),
        check_vma=False,
    )
```

```python
import jax
import jax.numpy as jnp
from jax import lax
from jax.experimental import pallas as pl
from jax.experimental.pallas import tpu as pltpu
from jax.sharding import PartitionSpec as P

BF16, F32 = jnp.bfloat16, jnp.float32
N = 4
BM = 512


def x_perm(d):
    return [(r, (r // N) * N + (r % N + d) % N) for r in range(N * N)]


def y_perm(d):
    return [(r, ((r // N + d) % N) * N + r % N) for r in range(N * N)]


def z_perm(d):
    return [(p, ((p // 2 + d) % N) * 2 + p % 2) for p in range(2 * N)]


SWAP = [(p, p ^ 1) for p in range(2 * N)]


def pick(index, choices):
    out = choices[0]
    for i in range(1, len(choices)):
        out = jnp.where(index == i, choices[i], out)
    return out


def after(value, *others):
    return lax.optimization_barrier((value,) + others)[0]


def params(mib):
    return pltpu.CompilerParams(vmem_limit_bytes=mib * 1024 * 1024)


def cost(flops, moved):
    return pl.CostEstimate(flops=int(flops), bytes_accessed=int(moved), transcendentals=0)


def whole():
    return pl.BlockSpec(memory_space=pltpu.VMEM)


def place_features(at, refs, dst, rows=None):
    z, core = at[2], at[3]
    for i, ref in enumerate(refs):
        zz = lax.rem(z + (0, 3, 1, 2)[i % 4], 4)
        cc = core if i < 4 else 1 - core
        off = pl.multiple_of((zz * 2 + cc) * 128, 128)
        dst[:, pl.ds(off, 128)] = ref[...]


def pack(at, env, low, p0, p1, p2, p3):
    n = env.shape[0] // 4
    for d, out in enumerate((p0, p1, p2, p3)):
        for i, add in enumerate((d, d + 2)):
            src = pl.ds(pl.multiple_of(lax.rem(at[0] + add, 4) * n, n), n)
            out[i * n : (i + 1) * n, :] = env[src, :]
            out[(i + 2) * n : (i + 3) * n, :] = low[src, :]


def kernel_slices(at, qt, s0, s1, s2, s3, s4, s5, s6, s7, k0, k1, low, feats):
    place_features(at, (s0, s1, s2, s3, s4, s5, s6, s7), feats)
    n = k0.shape[0]
    low[...] = feats[2 * n :, :]
    scale = 1.0 / (qt.shape[0] ** 0.5)
    dots = jnp.dot(feats[: 2 * n, :], qt[...], preferred_element_type=F32) * scale
    k = dots * dots
    k0[...] = k[:n].astype(BF16)
    k1[...] = k[n:]


def place_rows(at, refs, dst):
    color = lax.rem(at[0] + 2 * at[1], 4)
    for add, ref in zip((0, 1, 3, 2), refs):
        off = pl.multiple_of(lax.rem(color + add, 4) * ref.shape[0], ref.shape[0])
        dst[pl.ds(off, ref.shape[0]), :] = ref[...]


def first_solve(at, a, b, c, d, inv, low, k1, s0, t, rhs):
    place_rows(at, (a, b, c, d), rhs)
    s0[...] = jnp.dot(inv[...], rhs[...], preferred_element_type=F32).astype(BF16)
    t[...] = (k1[...] - jnp.dot(low[...], s0[...], preferred_element_type=F32)).astype(BF16)


def kernel_rows(at, qt, p0, p1, p2, p3, p4, p5, p6, p7, out, feats):
    place_features(at, (p0, p1, p2, p3, p4, p5, p6, p7), feats)
    scale = 1.0 / (qt.shape[0] ** 0.5)
    dots = jnp.dot(feats[...], qt[...], preferred_element_type=F32) * scale
    out[...] = dots * dots


def update(s0, low, k, out):
    out[...] = k[...] - jnp.dot(low[...], s0[...], preferred_element_type=F32)


def last_step(at, a, b, c, d, inv, s0, low, res, out, rhs, s1):
    i = pl.program_id(0)
    here = at[0] + 4 * at[1]
    bm = out.shape[0]
    per_block = s1.shape[0] // bm

    @pl.when(i == 0)
    def _():
        place_rows(at, (a, b, c, d), rhs)

        s1[...] = jnp.dot(inv[...], rhs[...], preferred_element_type=F32).astype(BF16)

    rows = pl.ds(pl.multiple_of(lax.rem(i, per_block) * bm, bm), bm)
    first = i < per_block

    @pl.when(jnp.logical_and(first, here == 0))
    def _():
        out[...] = s0[rows, :]

    @pl.when(jnp.logical_and(first, here == 1))
    def _():
        out[...] = s1[rows, :]

    @pl.when(jnp.logical_not(jnp.logical_and(first, here < 2)))
    def _():
        out[...] = (res[...] - jnp.dot(low[...], s1[...], preferred_element_type=F32)).astype(BF16)


def per_device(lower_panel, sparse_desc, query_desc, diag_inv):
    blocks, width, _ = lower_panel.shape
    queries = query_desc.shape[0]
    here, part = lax.axis_index("rows"), lax.axis_index("pb")
    x, y = here % N, here // N
    z, core = part // 2, part % 2
    at = jnp.stack([x, y, z, core]).astype(jnp.int32)
    smem = pl.BlockSpec(memory_space=pltpu.SMEM)
    quarter = width // 4
    piece = sparse_desc.shape[2]
    feats = piece * 2 * N

    qt = query_desc.T
    spread = jnp.broadcast_to(qt[None], (N * N,) + qt.shape)
    qt = lax.all_to_all(spread, "rows", 0, 0, tiled=True).reshape(feats, queries)

    got = pl.pallas_call(
        pack,
        grid_spec=pltpu.PrefetchScalarGridSpec(
            num_scalar_prefetch=1,
            grid=(1,),
            in_specs=[
                pl.BlockSpec((None, width, piece), lambda i, at: (0, 0, 0)),
                pl.BlockSpec((None, width, piece), lambda i, at: (0, 0, at[2] * 2 + at[3])),
            ],
            out_specs=[pl.BlockSpec((width, piece), lambda i, at: (0, 0))] * 4,
        ),
        out_shape=[jax.ShapeDtypeStruct((width, piece), BF16)] * 4,
        compiler_params=params(16),
    )(after(at, spread), sparse_desc, lower_panel)
    got = [got[0]] + [
        lax.ppermute(got[d], "rows", [(0, d), (1, (1 + d) % N)]) for d in (1, 2, 3)
    ]
    from0 = pick(x, got)
    from1 = pick((x + 3) % N, got)
    n = quarter
    even = jnp.concatenate([from0[:n], from1[:n], from1[2 * n : 3 * n]])
    odd = jnp.concatenate([from0[n : 2 * n], from1[n : 2 * n], from1[3 * n :]])
    got_y = [even] + [
        lax.ppermute(even if d == 2 else odd, "rows", [(c, d * N + c) for c in range(N)])
        for d in (1, 2, 3)
    ]
    mine = pick(y, got_y)
    slices = [mine] + [lax.ppermute(mine, "pb", z_perm(d)) for d in (1, -1, 2)]
    slices = slices + [lax.ppermute(v, "pb", SWAP) for v in slices]

    own = sparse_desc.reshape(blocks * width, piece)
    envs = [own] + [lax.ppermute(own, "pb", z_perm(d)) for d in (1, -1)]
    envs = envs + [lax.ppermute(after(own, envs[1]), "pb", z_perm(2))]
    envs = envs + [lax.ppermute(v, "pb", SWAP) for v in envs]

    unit = 2 * width * feats * queries
    k0, k1, low = pl.pallas_call(
        kernel_slices,
        out_shape=(
            jax.ShapeDtypeStruct((quarter, queries), BF16),
            jax.ShapeDtypeStruct((quarter, queries), F32),
            jax.ShapeDtypeStruct((quarter, width), BF16),
        ),
        in_specs=[smem] + [whole()] * 9,
        out_specs=(whole(),) * 3,
        scratch_shapes=[pltpu.VMEM((3 * quarter, feats), BF16)],
        compiler_params=params(16),
        cost_estimate=cost(unit / 2, 5e6),
    )(at, qt, *slices)

    def neighbours(v):
        return (
            v,
            lax.ppermute(v, "rows", x_perm(-1)),
            lax.ppermute(v, "rows", x_perm(1)),
            lax.ppermute(v, "rows", y_perm(-1)),
        )

    block = pl.BlockSpec((None, width, width), lambda *_: (0, 0, 0), memory_space=pltpu.VMEM)
    s0, t = pl.pallas_call(
        first_solve,
        grid=(1,),
        out_shape=(
            jax.ShapeDtypeStruct((width, queries), BF16),
            jax.ShapeDtypeStruct((quarter, queries), BF16),
        ),
        in_specs=[smem] + [whole()] * 4 + [block] + [whole()] * 2,
        out_specs=(whole(), whole()),
        scratch_shapes=[pltpu.VMEM((width, queries), BF16)],
        compiler_params=params(20),
        cost_estimate=cost(unit * 1.25, 8e6),
    )(at, *neighbours(k0), diag_inv, low, k1)

    bm = BM
    rows = blocks * width
    panel = lower_panel.reshape(rows, 2 * width)
    k_rows = pl.pallas_call(
        kernel_rows,
        grid=(rows // bm,),
        out_shape=jax.ShapeDtypeStruct((rows, queries), F32),
        in_specs=[smem, whole()] + [pl.BlockSpec((bm, piece), lambda i: (i, 0))] * 8,
        out_specs=pl.BlockSpec((bm, queries), lambda i: (i, 0)),
        scratch_shapes=[pltpu.VMEM((bm, feats), BF16)],
        compiler_params=params(16),
        cost_estimate=cost(unit * 2, 14e6),
    )(at, qt, *envs)
    res = pl.pallas_call(
        update,
        grid=(rows // bm,),
        out_shape=jax.ShapeDtypeStruct((rows, queries), F32),
        in_specs=[
            whole(),
            pl.BlockSpec((bm, width), lambda i: (i, 0)),
            pl.BlockSpec((bm, queries), lambda i: (i, 0)),
        ],
        out_specs=pl.BlockSpec((bm, queries), lambda i: (i, 0)),
        compiler_params=params(16),
        cost_estimate=cost(unit * 2, 22e6),
    )(s0, panel, k_rows)

    block1 = pl.BlockSpec((None, width, width), lambda *_: (1, 0, 0), memory_space=pltpu.VMEM)
    out = pl.pallas_call(
        last_step,
        grid=(rows // bm,),
        out_shape=jax.ShapeDtypeStruct((rows, queries), BF16),
        in_specs=[smem]
        + [whole()] * 4
        + [
            block1,
            whole(),
            pl.BlockSpec((bm, width), lambda i: (i, 1)),
            pl.BlockSpec((bm, queries), lambda i: (i, 0)),
        ],
        out_specs=pl.BlockSpec((bm, queries), lambda i: (i, 0)),
        scratch_shapes=[pltpu.VMEM((width, queries), BF16), pltpu.VMEM((width, queries), BF16)],
        compiler_params=params(20),
        cost_estimate=cost(unit * 3, 20e6),
    )(at, *neighbours(t), diag_inv, s0, panel, res)
    return out.reshape(blocks, width, queries)


def solution(mesh):
    return jax.shard_map(
        per_device,
        mesh=mesh,
        in_specs=(P(None, "rows", None), P(None, "rows", "pb"), P("pb", "rows"), P()),
        out_specs=P(None, "rows", "pb"),
        check_vma=False,
    )
```

```python
import jax
import jax.numpy as jnp
from jax import lax
from jax.experimental import pallas as pl
from jax.experimental.pallas import tpu as pltpu
from jax.sharding import PartitionSpec as P

BF16, F32 = jnp.bfloat16, jnp.float32
N = 4
BM = 512


def x_perm(d):
    return [(r, (r // N) * N + (r % N + d) % N) for r in range(N * N)]


def y_perm(d):
    return [(r, ((r // N + d) % N) * N + r % N) for r in range(N * N)]


def z_perm(d):
    return [(p, ((p // 2 + d) % N) * 2 + p % 2) for p in range(2 * N)]


SWAP = [(p, p ^ 1) for p in range(2 * N)]


def pick(index, choices):
    out = choices[0]
    for i in range(1, len(choices)):
        out = jnp.where(index == i, choices[i], out)
    return out


def after(value, *others):
    return lax.optimization_barrier((value,) + others)[0]


def params(mib):
    return pltpu.CompilerParams(vmem_limit_bytes=mib * 1024 * 1024)


def cost(flops, moved):
    return pl.CostEstimate(flops=int(flops), bytes_accessed=int(moved), transcendentals=0)


def whole():
    return pl.BlockSpec(memory_space=pltpu.VMEM)


def feature_offset(z, core, i):
    zz = lax.rem(z + (0, 3, 1, 2)[i % 4], 4)
    cc = core if i < 4 else 1 - core
    return pl.multiple_of((zz * 2 + cc) * 128, 128)


def place_features(at, refs, dst):
    for i, ref in enumerate(refs):
        dst[:, pl.ds(feature_offset(at[2], at[3], i), 128)] = ref[...]


def pack(at, env, low, qt, p0, p1, p2, p3, spread, sems):
    copies = [
        pltpu.make_async_copy(qt, spread.at[i], sems.at[i]) for i in range(spread.shape[0])
    ]
    for copy in copies:
        copy.start()
    n = env.shape[0] // 4
    for d, out in enumerate((p0, p1, p2, p3)):
        for i, add in enumerate((d, d + 2)):
            src = pl.ds(pl.multiple_of(lax.rem(at[0] + add, 4) * n, n), n)
            out[i * n : (i + 1) * n, :] = env[src, :]
            out[(i + 2) * n : (i + 3) * n, :] = low[src, :]
    for copy in copies:
        copy.wait()


def kernel_slices(at, qt, pieces, k0, k1, low, feats, sems):
    z, core = at[2], at[3]
    copies = []
    for i in range(pieces.shape[0]):
        off = feature_offset(z, core, i)
        copies.append(pltpu.make_async_copy(pieces.at[i], feats.at[:, pl.ds(off, 128)], sems.at[i]))
    for copy in copies:
        copy.start()
    for copy in copies:
        copy.wait()
    n = k0.shape[0]
    low[...] = feats[2 * n :, :]
    scale = 1.0 / (qt.shape[0] ** 0.5)
    dots = jnp.dot(feats[: 2 * n, :], qt[...], preferred_element_type=F32) * scale
    k = dots * dots
    k0[...] = k[:n].astype(BF16)
    k1[...] = k[n:]


def place_rows(at, refs, dst):
    color = lax.rem(at[0] + 2 * at[1], 4)
    for add, ref in zip((0, 1, 3, 2), refs):
        off = pl.multiple_of(lax.rem(color + add, 4) * ref.shape[0], ref.shape[0])
        dst[pl.ds(off, ref.shape[0]), :] = ref[...]


def first_solve(at, a, b, c, d, inv, low, k1, s0, t, rhs):
    place_rows(at, (a, b, c, d), rhs)
    s0[...] = jnp.dot(inv[...], rhs[...], preferred_element_type=F32).astype(BF16)
    t[...] = (k1[...] - jnp.dot(low[...], s0[...], preferred_element_type=F32)).astype(BF16)


def kernel_rows(at, qt, p0, p1, p2, p3, p4, p5, p6, p7, out, feats):
    place_features(at, (p0, p1, p2, p3, p4, p5, p6, p7), feats)
    scale = 1.0 / (qt.shape[0] ** 0.5)
    dots = jnp.dot(feats[...], qt[...], preferred_element_type=F32) * scale
    out[...] = dots * dots


def update(s0, low, k, out):
    out[...] = k[...] - jnp.dot(low[...], s0[...], preferred_element_type=F32)


def last_step(at, a, b, c, d, inv, s0, low, res, out, rhs, s1):
    i = pl.program_id(0)
    here = at[0] + 4 * at[1]
    bm = out.shape[0]
    per_block = s1.shape[0] // bm

    @pl.when(i == 0)
    def _():
        place_rows(at, (a, b, c, d), rhs)

        s1[...] = jnp.dot(inv[...], rhs[...], preferred_element_type=F32).astype(BF16)

    rows = pl.ds(pl.multiple_of(lax.rem(i, per_block) * bm, bm), bm)
    first = i < per_block

    @pl.when(jnp.logical_and(first, here == 0))
    def _():
        out[...] = s0[rows, :]

    @pl.when(jnp.logical_and(first, here == 1))
    def _():
        out[...] = s1[rows, :]

    @pl.when(jnp.logical_not(jnp.logical_and(first, here < 2)))
    def _():
        out[...] = (res[...] - jnp.dot(low[...], s1[...], preferred_element_type=F32)).astype(BF16)


def per_device(lower_panel, sparse_desc, query_desc, diag_inv):
    blocks, width, _ = lower_panel.shape
    queries = query_desc.shape[0]
    here, part = lax.axis_index("rows"), lax.axis_index("pb")
    x, y = here % N, here // N
    z, core = part // 2, part % 2
    at = jnp.stack([x, y, z, core]).astype(jnp.int32)
    smem = pl.BlockSpec(memory_space=pltpu.SMEM)
    quarter = width // 4
    piece = sparse_desc.shape[2]
    feats = piece * 2 * N

    own_q = query_desc.T
    *got, spread = pl.pallas_call(
        pack,
        grid_spec=pltpu.PrefetchScalarGridSpec(
            num_scalar_prefetch=1,
            grid=(1,),
            in_specs=[
                pl.BlockSpec((None, width, piece), lambda i, at: (0, 0, 0)),
                pl.BlockSpec((None, width, piece), lambda i, at: (0, 0, at[2] * 2 + at[3])),
                pl.BlockSpec(own_q.shape, lambda i, at: (0, 0)),
            ],
            out_specs=[pl.BlockSpec((width, piece), lambda i, at: (0, 0))] * 4
            + [pl.BlockSpec(memory_space=pl.ANY)],
            scratch_shapes=[pltpu.SemaphoreType.DMA((N * N,))],
        ),
        out_shape=[jax.ShapeDtypeStruct((width, piece), BF16)] * 4
        + [jax.ShapeDtypeStruct((N * N,) + own_q.shape, BF16)],
        compiler_params=params(56),
    )(at, sparse_desc, lower_panel, own_q)
    qt = lax.all_to_all(spread, "rows", 0, 0, tiled=True).reshape(feats, queries)
    own = sparse_desc.reshape(blocks * width, piece)
    early = after(own, got[0])
    envs = [own] + [lax.ppermute(early, "pb", z_perm(d)) for d in (1, -1)]
    envs = envs + [lax.ppermute(after(own, envs[1]), "pb", z_perm(2))]
    envs = envs + [lax.ppermute(v, "pb", SWAP) for v in envs]

    got = [got[0]] + [
        lax.ppermute(got[d], "rows", [(0, d), (1, (1 + d) % N)]) for d in (1, 2, 3)
    ]
    from0 = pick(x, got)
    from1 = pick((x + 3) % N, got)
    n = quarter
    even = jnp.concatenate([from0[:n], from1[:n], from1[2 * n : 3 * n]])
    odd = jnp.concatenate([from0[n : 2 * n], from1[n : 2 * n], from1[3 * n :]])
    even, odd, _, _ = lax.optimization_barrier((even, odd, envs[1], envs[2]))
    got_y = [even] + [
        lax.ppermute(even if d == 2 else odd, "rows", [(c, d * N + c) for c in range(N)])
        for d in (1, 2, 3)
    ]
    mine = pick(y, got_y)
    mine = after(mine, envs[3])
    slices = [mine] + [lax.ppermute(mine, "pb", z_perm(d)) for d in (1, -1, 2)]
    slices = slices + [lax.ppermute(v, "pb", SWAP) for v in slices]

    unit = 2 * width * feats * queries
    k0, k1, low = pl.pallas_call(
        kernel_slices,
        out_shape=(
            jax.ShapeDtypeStruct((quarter, queries), BF16),
            jax.ShapeDtypeStruct((quarter, queries), F32),
            jax.ShapeDtypeStruct((quarter, width), BF16),
        ),
        in_specs=[smem, whole(), pl.BlockSpec(memory_space=pl.ANY)],
        out_specs=(whole(),) * 3,
        scratch_shapes=[pltpu.VMEM((3 * quarter, feats), BF16), pltpu.SemaphoreType.DMA((8,))],
        compiler_params=params(56),
        cost_estimate=cost(unit / 2, 5e6),
    )(at, qt, jnp.stack(slices))

    def neighbours(v):
        return (
            v,
            lax.ppermute(v, "rows", x_perm(-1)),
            lax.ppermute(v, "rows", x_perm(1)),
            lax.ppermute(v, "rows", y_perm(-1)),
        )

    block = pl.BlockSpec((None, width, width), lambda *_: (0, 0, 0), memory_space=pltpu.VMEM)
    s0, t = pl.pallas_call(
        first_solve,
        grid=(1,),
        out_shape=(
            jax.ShapeDtypeStruct((width, queries), BF16),
            jax.ShapeDtypeStruct((quarter, queries), BF16),
        ),
        in_specs=[smem] + [whole()] * 4 + [block] + [whole()] * 2,
        out_specs=(whole(), whole()),
        scratch_shapes=[pltpu.VMEM((width, queries), BF16)],
        compiler_params=params(20),
        cost_estimate=cost(unit * 1.25, 8e6),
    )(at, *neighbours(k0), diag_inv, low, k1)

    bm = BM
    rows = blocks * width
    panel = lower_panel.reshape(rows, 2 * width)
    k_rows = pl.pallas_call(
        kernel_rows,
        grid=(rows // bm,),
        out_shape=jax.ShapeDtypeStruct((rows, queries), F32),
        in_specs=[smem, whole()] + [pl.BlockSpec((bm, piece), lambda i: (i, 0))] * 8,
        out_specs=pl.BlockSpec((bm, queries), lambda i: (i, 0)),
        scratch_shapes=[pltpu.VMEM((bm, feats), BF16)],
        compiler_params=params(16),
        cost_estimate=cost(unit * 2, 14e6),
    )(at, qt, *envs)
    res = pl.pallas_call(
        update,
        grid=(rows // bm,),
        out_shape=jax.ShapeDtypeStruct((rows, queries), F32),
        in_specs=[
            whole(),
            pl.BlockSpec((bm, width), lambda i: (i, 0)),
            pl.BlockSpec((bm, queries), lambda i: (i, 0)),
        ],
        out_specs=pl.BlockSpec((bm, queries), lambda i: (i, 0)),
        compiler_params=params(16),
        cost_estimate=cost(unit * 2, 22e6),
    )(s0, panel, k_rows)

    block1 = pl.BlockSpec((None, width, width), lambda *_: (1, 0, 0), memory_space=pltpu.VMEM)
    out = pl.pallas_call(
        last_step,
        grid=(rows // bm,),
        out_shape=jax.ShapeDtypeStruct((rows, queries), BF16),
        in_specs=[smem]
        + [whole()] * 4
        + [
            block1,
            whole(),
            pl.BlockSpec((bm, width), lambda i: (i, 1)),
            pl.BlockSpec((bm, queries), lambda i: (i, 0)),
        ],
        out_specs=pl.BlockSpec((bm, queries), lambda i: (i, 0)),
        scratch_shapes=[pltpu.VMEM((width, queries), BF16), pltpu.VMEM((width, queries), BF16)],
        compiler_params=params(20),
        cost_estimate=cost(unit * 3, 20e6),
    )(at, *neighbours(t), diag_inv, s0, panel, res)
    return out.reshape(blocks, width, queries)


def solution(mesh):
    return jax.shard_map(
        per_device,
        mesh=mesh,
        in_specs=(P(None, "rows", None), P(None, "rows", "pb"), P("pb", "rows"), P()),
        out_specs=P(None, "rows", "pb"),
        check_vma=False,
    )
```

```python
import jax
import jax.numpy as jnp
from jax import lax
from jax.experimental import pallas as pl
from jax.experimental.pallas import tpu as pltpu
from jax.sharding import PartitionSpec as P

BF16, F32 = jnp.bfloat16, jnp.float32
N = 4
BM = 512


def x_perm(d):
    return [(r, (r // N) * N + (r % N + d) % N) for r in range(N * N)]


def y_perm(d):
    return [(r, ((r // N + d) % N) * N + r % N) for r in range(N * N)]


def z_perm(d):
    return [(p, ((p // 2 + d) % N) * 2 + p % 2) for p in range(2 * N)]


SWAP = [(p, p ^ 1) for p in range(2 * N)]


def pick(index, choices):
    out = choices[0]
    for i in range(1, len(choices)):
        out = jnp.where(index == i, choices[i], out)
    return out


def after(value, *others):
    return lax.optimization_barrier((value,) + others)[0]


def params(mib):
    return pltpu.CompilerParams(vmem_limit_bytes=mib * 1024 * 1024)


def cost(flops, moved):
    return pl.CostEstimate(flops=int(flops), bytes_accessed=int(moved), transcendentals=0)


def whole():
    return pl.BlockSpec(memory_space=pltpu.VMEM)


def feature_offset(z, core, i):
    zz = lax.rem(z + (0, 3, 1, 2)[i % 4], 4)
    cc = core if i < 4 else 1 - core
    return pl.multiple_of((zz * 2 + cc) * 128, 128)


def place_features(at, refs, dst):
    for i, ref in enumerate(refs):
        dst[:, pl.ds(feature_offset(at[2], at[3], i), 128)] = ref[...]


def spread(src, dst, sems):
    copies = [pltpu.make_async_copy(src, dst.at[i], sems.at[i]) for i in range(dst.shape[0])]
    for copy in copies:
        copy.start()
    for copy in copies:
        copy.wait()


def pack(at, env, low, p0, p1, p2, p3):
    n = env.shape[0] // 4
    for d, out in enumerate((p0, p1, p2, p3)):
        for i, add in enumerate((d, d + 2)):
            src = pl.ds(pl.multiple_of(lax.rem(at[0] + add, 4) * n, n), n)
            out[i * n : (i + 1) * n, :] = env[src, :]
            out[(i + 2) * n : (i + 3) * n, :] = low[src, :]


def assemble(at, p0, p1, p2, p3, p4, p5, p6, p7, feats, low):
    n = low.shape[0]
    for i, ref in enumerate((p0, p1, p2, p3, p4, p5, p6, p7)):
        cols = pl.ds(feature_offset(at[2], at[3], i), 128)
        feats[:, cols] = ref[: 2 * n, :]
        low[:, cols] = ref[2 * n :, :]


def through_first(low, inv, high, rest):
    both = jnp.dot(low[...], inv[...], preferred_element_type=F32)
    high[...] = both.astype(BF16)
    rest[...] = (both - high[...].astype(F32)).astype(BF16)


def square(feats, qt, total):
    dots = jnp.dot(feats, qt, preferred_element_type=F32) * (1.0 / (total**0.5))
    return dots * dots


def kernel_slices(feats, qa, qb, k0, k1):
    n, half = k0.shape[0], qa.shape[1]
    for i, q in enumerate((qa, qb)):
        cols = slice(i * half, (i + 1) * half)
        k = square(feats[...], q[...], qa.shape[0])
        k0[:, cols] = k[:n].astype(BF16)
        k1[:, cols] = k[n:]


def place_rows(at, refs, dst):
    color = lax.rem(at[0] + 2 * at[1], 4)
    for add, ref in zip((0, 1, 3, 2), refs):
        off = pl.multiple_of(lax.rem(color + add, 4) * ref.shape[0], ref.shape[0])
        dst[pl.ds(off, ref.shape[0]), :] = ref[...]


def right_side(at, a, b, c, d, high, rest, k1, t, rhs):
    place_rows(at, (a, b, c, d), rhs)
    low = jnp.dot(high[...], rhs[...], preferred_element_type=F32)
    low = low + jnp.dot(rest[...], rhs[...], preferred_element_type=F32)
    t[...] = (k1[...] - low).astype(BF16)


def first_solve(rhs, inv, s0):
    s0[...] = jnp.dot(inv[...], rhs[...], preferred_element_type=F32).astype(BF16)


def kernel_rows(at, qa, qb, p0, p1, p2, p3, p4, p5, p6, p7, out, feats):
    place_features(at, (p0, p1, p2, p3, p4, p5, p6, p7), feats)
    half = qa.shape[1]
    for i, q in enumerate((qa, qb)):
        out[:, i * half : (i + 1) * half] = square(feats[...], q[...], qa.shape[0])


def update(s0, low, k, out):
    out[...] = k[...] - jnp.dot(low[...], s0[...], preferred_element_type=F32)


def last_step(at, a, b, c, d, inv, s0, low, res, out, rhs, s1):
    i = pl.program_id(0)
    here = at[0] + 4 * at[1]
    bm = out.shape[0]
    per_block = s1.shape[0] // bm

    @pl.when(i == 0)
    def _():
        place_rows(at, (a, b, c, d), rhs)

        s1[...] = jnp.dot(inv[...], rhs[...], preferred_element_type=F32).astype(BF16)

    rows = pl.ds(pl.multiple_of(lax.rem(i, per_block) * bm, bm), bm)
    first = i < per_block

    @pl.when(jnp.logical_and(first, here == 0))
    def _():
        out[...] = s0[rows, :]

    @pl.when(jnp.logical_and(first, here == 1))
    def _():
        out[...] = s1[rows, :]

    @pl.when(jnp.logical_not(jnp.logical_and(first, here < 2)))
    def _():
        out[...] = (res[...] - jnp.dot(low[...], s1[...], preferred_element_type=F32)).astype(BF16)


def per_device(lower_panel, sparse_desc, query_desc, diag_inv):
    blocks, width, _ = lower_panel.shape
    queries = query_desc.shape[0]
    here, part = lax.axis_index("rows"), lax.axis_index("pb")
    x, y = here % N, here // N
    z, core = part // 2, part % 2
    at = jnp.stack([x, y, z, core]).astype(jnp.int32)
    smem = pl.BlockSpec(memory_space=pltpu.SMEM)
    quarter = width // 4
    piece = sparse_desc.shape[2]
    feats = piece * 2 * N

    got = pl.pallas_call(
        pack,
        grid_spec=pltpu.PrefetchScalarGridSpec(
            num_scalar_prefetch=1,
            grid=(1,),
            in_specs=[
                pl.BlockSpec((None, width, piece), lambda i, at: (0, 0, 0)),
                pl.BlockSpec((None, width, piece), lambda i, at: (0, 0, at[2] * 2 + at[3])),
            ],
            out_specs=[pl.BlockSpec((width, piece), lambda i, at: (0, 0))] * 4,
        ),
        out_shape=[jax.ShapeDtypeStruct((width, piece), BF16)] * 4,
        compiler_params=params(56),
    )(at, sparse_desc, lower_panel)

    own_q = query_desc.T
    half = queries // 2

    def gather_queries(part, source):
        block = pl.BlockSpec((own_q.shape[0], half), lambda i: (0, part))
        copies = pl.pallas_call(
            spread,
            grid=(1,),
            in_specs=[block],
            out_specs=pl.BlockSpec(memory_space=pl.ANY),
            out_shape=jax.ShapeDtypeStruct((N * N, own_q.shape[0], half), BF16),
            scratch_shapes=[pltpu.SemaphoreType.DMA((N * N,))],
            compiler_params=params(56),
        )(source)
        return lax.all_to_all(copies, "rows", 0, 0, tiled=True).reshape(feats, half)

    qa = gather_queries(0, after(own_q, got[0]))

    own = sparse_desc.reshape(blocks * width, piece)
    envs = [own] + [lax.ppermute(own, "pb", z_perm(d)) for d in (1, -1, 2)]
    envs = envs + [lax.ppermute(v, "pb", SWAP) for v in envs]

    got = [got[0]] + [
        lax.ppermute(got[d], "rows", [(0, d), (1, (1 + d) % N)]) for d in (1, 2, 3)
    ]
    from0 = pick(x, got)
    from1 = pick((x + 3) % N, got)
    n = quarter
    even = jnp.concatenate([from0[:n], from1[:n], from1[2 * n : 3 * n]])
    odd = jnp.concatenate([from0[n : 2 * n], from1[n : 2 * n], from1[3 * n :]])
    qb = gather_queries(1, after(own_q, even))
    got_y = [even] + [
        lax.ppermute(even if d == 2 else odd, "rows", [(c, d * N + c) for c in range(N)])
        for d in (1, 2, 3)
    ]
    mine = pick(y, got_y)
    mine, _, _, _ = lax.optimization_barrier((mine, envs[1], envs[2], envs[3]))
    slices = [mine] + [lax.ppermute(mine, "pb", z_perm(d)) for d in (1, -1, 2)]
    slices = slices + [lax.ppermute(v, "pb", SWAP) for v in slices]

    unit = 2 * width * feats * queries
    def block(i):
        return pl.BlockSpec((None, width, width), lambda *_: (i, 0, 0))

    narrow = jax.ShapeDtypeStruct((quarter, width), BF16)
    slice_feats, low = pl.pallas_call(
        assemble,
        out_shape=(jax.ShapeDtypeStruct((2 * quarter, feats), BF16), narrow),
        in_specs=[smem] + [whole()] * 8,
        out_specs=(whole(),) * 2,
        compiler_params=params(16),
    )(at, *slices)
    k0, k1 = pl.pallas_call(
        kernel_slices,
        out_shape=(
            jax.ShapeDtypeStruct((quarter, queries), BF16),
            jax.ShapeDtypeStruct((quarter, queries), F32),
        ),
        in_specs=[whole()] * 3,
        out_specs=(whole(), whole()),
        compiler_params=params(16),
        cost_estimate=cost(unit / 2, 5e6),
    )(slice_feats, qa, qb)

    high, rest = pl.pallas_call(
        through_first,
        grid=(1,),
        out_shape=(narrow, narrow),
        in_specs=[whole(), block(0)],
        out_specs=(whole(),) * 2,
        compiler_params=params(16),
        cost_estimate=cost(unit / 4, 5e6),
    )(after(low, k0), diag_inv)

    def neighbours(v):
        return (
            v,
            lax.ppermute(v, "rows", x_perm(-1)),
            lax.ppermute(v, "rows", x_perm(1)),
            lax.ppermute(v, "rows", y_perm(-1)),
        )

    t, rhs = pl.pallas_call(
        right_side,
        out_shape=(
            jax.ShapeDtypeStruct((quarter, queries), BF16),
            jax.ShapeDtypeStruct((width, queries), BF16),
        ),
        in_specs=[smem] + [whole()] * 7,
        out_specs=(whole(),) * 2,
        compiler_params=params(20),
        cost_estimate=cost(unit * 0.5, 8e6),
    )(at, *neighbours(k0), high, rest, k1)
    s0 = pl.pallas_call(
        first_solve,
        grid=(1,),
        out_shape=jax.ShapeDtypeStruct((width, queries), BF16),
        in_specs=[whole(), block(0)],
        out_specs=whole(),
        compiler_params=params(20),
        cost_estimate=cost(unit, 6e6),
    )(rhs, diag_inv)

    bm = BM
    rows = blocks * width
    panel = lower_panel.reshape(rows, 2 * width)
    k_rows = pl.pallas_call(
        kernel_rows,
        grid=(rows // bm,),
        out_shape=jax.ShapeDtypeStruct((rows, queries), F32),
        in_specs=[smem, whole(), whole()] + [pl.BlockSpec((bm, piece), lambda i: (i, 0))] * 8,
        out_specs=pl.BlockSpec((bm, queries), lambda i: (i, 0)),
        scratch_shapes=[pltpu.VMEM((bm, feats), BF16)],
        compiler_params=params(16),
        cost_estimate=cost(unit * 2, 14e6),
    )(at, qa, qb, *envs)
    res = pl.pallas_call(
        update,
        grid=(rows // bm,),
        out_shape=jax.ShapeDtypeStruct((rows, queries), F32),
        in_specs=[
            whole(),
            pl.BlockSpec((bm, width), lambda i: (i, 0)),
            pl.BlockSpec((bm, queries), lambda i: (i, 0)),
        ],
        out_specs=pl.BlockSpec((bm, queries), lambda i: (i, 0)),
        compiler_params=params(16),
        cost_estimate=cost(unit * 2, 22e6),
    )(s0, panel, k_rows)

    out = pl.pallas_call(
        last_step,
        grid=(rows // bm,),
        out_shape=jax.ShapeDtypeStruct((rows, queries), BF16),
        in_specs=[smem]
        + [whole()] * 4
        + [
            block(1),
            whole(),
            pl.BlockSpec((bm, width), lambda i: (i, 1)),
            pl.BlockSpec((bm, queries), lambda i: (i, 0)),
        ],
        out_specs=pl.BlockSpec((bm, queries), lambda i: (i, 0)),
        scratch_shapes=[pltpu.VMEM((width, queries), BF16), pltpu.VMEM((width, queries), BF16)],
        compiler_params=params(20),
        cost_estimate=cost(unit * 3, 20e6),
    )(at, *neighbours(t), diag_inv, s0, panel, res)
    return out.reshape(blocks, width, queries)


def solution(mesh):
    return jax.shard_map(
        per_device,
        mesh=mesh,
        in_specs=(P(None, "rows", None), P(None, "rows", "pb"), P("pb", "rows"), P()),
        out_specs=P(None, "rows", "pb"),
        check_vma=False,
    )
```

```python
import functools

import jax
import jax.numpy as jnp
from jax import lax
from jax.experimental import pallas as pl
from jax.experimental.pallas import tpu as pltpu
from jax.sharding import PartitionSpec as P

BF16, F32 = jnp.bfloat16, jnp.float32
N = 4
BM = 512


def x_perm(d):
    return [(r, (r // N) * N + (r % N + d) % N) for r in range(N * N)]


def y_perm(d):
    return [(r, ((r // N + d) % N) * N + r % N) for r in range(N * N)]


def z_perm(d):
    return [(p, ((p // 2 + d) % N) * 2 + p % 2) for p in range(2 * N)]


SWAP = [(p, p ^ 1) for p in range(2 * N)]


def pick(index, choices):
    out = choices[0]
    for i in range(1, len(choices)):
        out = jnp.where(index == i, choices[i], out)
    return out


def after(value, *others):
    return lax.optimization_barrier((value,) + others)[0]


def params(mib):
    return pltpu.CompilerParams(vmem_limit_bytes=mib * 1024 * 1024)


def cost(flops, moved):
    return pl.CostEstimate(flops=int(flops), bytes_accessed=int(moved), transcendentals=0)


def whole():
    return pl.BlockSpec(memory_space=pltpu.VMEM)


def feature_offset(z, core, i):
    zz = lax.rem(z + (0, 3, 1, 2)[i % 4], 4)
    cc = core if i < 4 else 1 - core
    return pl.multiple_of((zz * 2 + cc) * 128, 128)


def place_features(at, refs, dst):
    for i, ref in enumerate(refs):
        dst[:, pl.ds(feature_offset(at[2], at[3], i), 128)] = ref[...]


def spread(start, src, dst, sems):
    part = src.at[:, start : start + dst.shape[2]]
    copies = [pltpu.make_async_copy(part, dst.at[i], sems.at[i]) for i in range(dst.shape[0])]
    for copy in copies:
        copy.start()
    for copy in copies:
        copy.wait()


def pack(at, env, low, p0, p1, p2, p3):
    n = env.shape[0] // 4
    for d, out in enumerate((p0, p1, p2, p3)):
        for i, add in enumerate((d, d + 2)):
            src = pl.ds(pl.multiple_of(lax.rem(at[0] + add, 4) * n, n), n)
            out[i * n : (i + 1) * n, :] = env[src, :]
            out[(i + 2) * n : (i + 3) * n, :] = low[src, :]


def assemble(at, p0, p1, p2, p3, p4, p5, p6, p7, feats, low):
    n = low.shape[0]
    for i, ref in enumerate((p0, p1, p2, p3, p4, p5, p6, p7)):
        cols = pl.ds(feature_offset(at[2], at[3], i), 128)
        feats[:, cols] = ref[: 2 * n, :]
        low[:, cols] = ref[2 * n :, :]


def through_first(low, inv, high, rest):
    both = jnp.dot(low[...], inv[...], preferred_element_type=F32)
    high[...] = both.astype(BF16)
    rest[...] = (both - high[...].astype(F32)).astype(BF16)


def square(feats, qt, total):
    dots = jnp.dot(feats, qt, preferred_element_type=F32) * (1.0 / (total**0.5))
    return dots * dots


def kernel_slices(feats, qa, qb, k0, k1):
    n, start = k0.shape[0], 0
    for q in (qa, qb):
        cols = slice(start, start + q.shape[1])
        k = square(feats[...], q[...], q.shape[0])
        k0[:, cols] = k[:n].astype(BF16)
        k1[:, cols] = k[n:]
        start += q.shape[1]


def place_rows(at, refs, dst):
    color = lax.rem(at[0] + 2 * at[1], 4)
    for add, ref in zip((0, 1, 3, 2), refs):
        off = pl.multiple_of(lax.rem(color + add, 4) * ref.shape[0], ref.shape[0])
        dst[pl.ds(off, ref.shape[0]), :] = ref[...]


def right_side(at, a, b, c, d, high, rest, k1, t, rhs):
    place_rows(at, (a, b, c, d), rhs)
    low = jnp.dot(high[...], rhs[...], preferred_element_type=F32)
    low = low + jnp.dot(rest[...], rhs[...], preferred_element_type=F32)
    t[...] = (k1[...] - low).astype(BF16)


def first_solve(rhs, inv, s0):
    s0[...] = jnp.dot(inv[...], rhs[...], preferred_element_type=F32).astype(BF16)


def kernel_rows(at, qa, qb, p0, p1, p2, p3, p4, p5, p6, p7, out, feats):
    place_features(at, (p0, p1, p2, p3, p4, p5, p6, p7), feats)
    start = 0
    for q in (qa, qb):
        out[:, start : start + q.shape[1]] = square(feats[...], q[...], q.shape[0])
        start += q.shape[1]


def update(s0, low, k, out):
    out[...] = k[...] - jnp.dot(low[...], s0[...], preferred_element_type=F32)


def last_step(at, a, b, c, d, inv, s0, low, res, out, rhs, s1):
    i = pl.program_id(0)
    here = at[0] + 4 * at[1]
    bm = out.shape[0]
    per_block = s1.shape[0] // bm

    @pl.when(i == 0)
    def _():
        place_rows(at, (a, b, c, d), rhs)

        s1[...] = jnp.dot(inv[...], rhs[...], preferred_element_type=F32).astype(BF16)

    rows = pl.ds(pl.multiple_of(lax.rem(i, per_block) * bm, bm), bm)
    first = i < per_block

    @pl.when(jnp.logical_and(first, here == 0))
    def _():
        out[...] = s0[rows, :]

    @pl.when(jnp.logical_and(first, here == 1))
    def _():
        out[...] = s1[rows, :]

    @pl.when(jnp.logical_not(jnp.logical_and(first, here < 2)))
    def _():
        out[...] = (res[...] - jnp.dot(low[...], s1[...], preferred_element_type=F32)).astype(BF16)


def per_device(lower_panel, sparse_desc, query_desc, diag_inv):
    blocks, width, _ = lower_panel.shape
    queries = query_desc.shape[0]
    here, part = lax.axis_index("rows"), lax.axis_index("pb")
    x, y = here % N, here // N
    z, core = part // 2, part % 2
    at = jnp.stack([x, y, z, core]).astype(jnp.int32)
    smem = pl.BlockSpec(memory_space=pltpu.SMEM)
    quarter = width // 4
    piece = sparse_desc.shape[2]
    feats = piece * 2 * N

    got = pl.pallas_call(
        pack,
        grid_spec=pltpu.PrefetchScalarGridSpec(
            num_scalar_prefetch=1,
            grid=(1,),
            in_specs=[
                pl.BlockSpec((None, width, piece), lambda i, at: (0, 0, 0)),
                pl.BlockSpec((None, width, piece), lambda i, at: (0, 0, at[2] * 2 + at[3])),
            ],
            out_specs=[pl.BlockSpec((width, piece), lambda i, at: (0, 0))] * 4,
        ),
        out_shape=[jax.ShapeDtypeStruct((width, piece), BF16)] * 4,
        compiler_params=params(56),
    )(at, sparse_desc, lower_panel)

    own_q = query_desc.T
    first_part = queries // 4

    def gather_queries(start, count, source):
        copies = pl.pallas_call(
            functools.partial(spread, start),
            in_specs=[whole()],
            out_specs=pl.BlockSpec(memory_space=pl.ANY),
            out_shape=jax.ShapeDtypeStruct((N * N, own_q.shape[0], count), BF16),
            scratch_shapes=[pltpu.SemaphoreType.DMA((N * N,))],
            compiler_params=params(56),
        )(source)
        return lax.all_to_all(copies, "rows", 0, 0, tiled=True).reshape(feats, count)

    qa = gather_queries(0, first_part, after(own_q, got[0]))

    own = sparse_desc.reshape(blocks * width, piece)
    early = after(own, got[0])
    envs = [own] + [lax.ppermute(early, "pb", z_perm(d)) for d in (1, -1)]

    got = [got[0]] + [
        lax.ppermute(got[d], "rows", [(0, d), (1, (1 + d) % N)]) for d in (1, 2, 3)
    ]
    from0 = pick(x, got)
    from1 = pick((x + 3) % N, got)
    n = quarter
    even = jnp.concatenate([from0[:n], from1[:n], from1[2 * n : 3 * n]])
    odd = jnp.concatenate([from0[n : 2 * n], from1[n : 2 * n], from1[3 * n :]])
    qb = gather_queries(first_part, queries - first_part, after(own_q, even))
    got_y = [even] + [
        lax.ppermute(even if d == 2 else odd, "rows", [(c, d * N + c) for c in range(N)])
        for d in (1, 2, 3)
    ]
    mine = pick(y, got_y)
    mine, _, _ = lax.optimization_barrier((mine, envs[1], envs[2]))
    slices = [mine] + [lax.ppermute(mine, "pb", z_perm(d)) for d in (1, -1, 2)]
    envs = envs + [lax.ppermute(after(own, slices[1]), "pb", z_perm(2))]
    slices = slices + [lax.ppermute(v, "pb", SWAP) for v in slices]

    unit = 2 * width * feats * queries
    def block(i):
        return pl.BlockSpec((None, width, width), lambda *_: (i, 0, 0))

    narrow = jax.ShapeDtypeStruct((quarter, width), BF16)
    slice_feats, low = pl.pallas_call(
        assemble,
        out_shape=(jax.ShapeDtypeStruct((2 * quarter, feats), BF16), narrow),
        in_specs=[smem] + [whole()] * 8,
        out_specs=(whole(),) * 2,
        compiler_params=params(16),
        cost_estimate=cost(6900000000, 22200000),
    )(at, *slices)
    k0, k1 = pl.pallas_call(
        kernel_slices,
        out_shape=(
            jax.ShapeDtypeStruct((quarter, queries), BF16),
            jax.ShapeDtypeStruct((quarter, queries), F32),
        ),
        in_specs=[whole()] * 3,
        out_specs=(whole(), whole()),
        compiler_params=params(16),
        cost_estimate=cost(unit / 2, 5e6),
    )(slice_feats, qa, qb)

    high, rest = pl.pallas_call(
        through_first,
        grid=(1,),
        out_shape=(narrow, narrow),
        in_specs=[whole(), block(0)],
        out_specs=(whole(),) * 2,
        compiler_params=params(16),
        cost_estimate=cost(unit / 4, 5e6),
    )(low, diag_inv)

    def neighbours(v):
        return (
            v,
            lax.ppermute(v, "rows", x_perm(-1)),
            lax.ppermute(v, "rows", x_perm(1)),
            lax.ppermute(v, "rows", y_perm(-1)),
        )

    t, rhs = pl.pallas_call(
        right_side,
        out_shape=(
            jax.ShapeDtypeStruct((quarter, queries), BF16),
            jax.ShapeDtypeStruct((width, queries), BF16),
        ),
        in_specs=[smem] + [whole()] * 7,
        out_specs=(whole(),) * 2,
        compiler_params=params(20),
        cost_estimate=cost(unit * 0.5, 8e6),
    )(at, *neighbours(k0), high, rest, k1)
    s0 = pl.pallas_call(
        first_solve,
        grid=(1,),
        out_shape=jax.ShapeDtypeStruct((width, queries), BF16),
        in_specs=[whole(), block(0)],
        out_specs=whole(),
        compiler_params=params(20),
        cost_estimate=cost(unit, 6e6),
    )(rhs, diag_inv)

    envs = envs + [lax.ppermute(v, "pb", SWAP) for v in (after(e, k0) for e in envs)]

    bm = BM
    rows = blocks * width
    panel = lower_panel.reshape(rows, 2 * width)
    k_rows = pl.pallas_call(
        kernel_rows,
        grid=(rows // bm,),
        out_shape=jax.ShapeDtypeStruct((rows, queries), F32),
        in_specs=[smem, whole(), whole()] + [pl.BlockSpec((bm, piece), lambda i: (i, 0))] * 8,
        out_specs=pl.BlockSpec((bm, queries), lambda i: (i, 0)),
        scratch_shapes=[pltpu.VMEM((bm, feats), BF16)],
        compiler_params=params(16),
        cost_estimate=cost(unit * 2, 14e6),
    )(at, qa, qb, *envs)
    res = pl.pallas_call(
        update,
        grid=(rows // bm,),
        out_shape=jax.ShapeDtypeStruct((rows, queries), F32),
        in_specs=[
            whole(),
            pl.BlockSpec((bm, width), lambda i: (i, 0)),
            pl.BlockSpec((bm, queries), lambda i: (i, 0)),
        ],
        out_specs=pl.BlockSpec((bm, queries), lambda i: (i, 0)),
        compiler_params=params(16),
        cost_estimate=cost(unit * 2, 22e6),
    )(s0, panel, k_rows)

    out = pl.pallas_call(
        last_step,
        grid=(rows // bm,),
        out_shape=jax.ShapeDtypeStruct((rows, queries), BF16),
        in_specs=[smem]
        + [whole()] * 4
        + [
            block(1),
            whole(),
            pl.BlockSpec((bm, width), lambda i: (i, 1)),
            pl.BlockSpec((bm, queries), lambda i: (i, 0)),
        ],
        out_specs=pl.BlockSpec((bm, queries), lambda i: (i, 0)),
        scratch_shapes=[pltpu.VMEM((width, queries), BF16), pltpu.VMEM((width, queries), BF16)],
        compiler_params=params(20),
        cost_estimate=cost(unit * 3, 20e6),
    )(at, *neighbours(t), diag_inv, s0, panel, res)
    return out.reshape(blocks, width, queries)


def solution(mesh):
    return jax.shard_map(
        per_device,
        mesh=mesh,
        in_specs=(P(None, "rows", None), P(None, "rows", "pb"), P("pb", "rows"), P()),
        out_specs=P(None, "rows", "pb"),
        check_vma=False,
    )
```

```python
import functools

import jax
import jax.numpy as jnp
from jax import lax
from jax.experimental import pallas as pl
from jax.experimental.pallas import tpu as pltpu
from jax.sharding import PartitionSpec as P

BF16, F32 = jnp.bfloat16, jnp.float32
N = 4
BM = 512


def x_perm(d):
    return [(r, (r // N) * N + (r % N + d) % N) for r in range(N * N)]


def y_perm(d):
    return [(r, ((r // N + d) % N) * N + r % N) for r in range(N * N)]


def z_perm(d):
    return [(p, ((p // 2 + d) % N) * 2 + p % 2) for p in range(2 * N)]


SWAP = [(p, p ^ 1) for p in range(2 * N)]


def pick(index, choices):
    out = choices[0]
    for i in range(1, len(choices)):
        out = jnp.where(index == i, choices[i], out)
    return out


def after(value, *others):
    return lax.optimization_barrier((value,) + others)[0]


def params(mib):
    return pltpu.CompilerParams(vmem_limit_bytes=mib * 1024 * 1024)


def cost(flops, moved):
    return pl.CostEstimate(flops=int(flops), bytes_accessed=int(moved), transcendentals=0)


def whole():
    return pl.BlockSpec(memory_space=pltpu.VMEM)


def feature_offset(z, core, i):
    zz = lax.rem(z + (0, 3, 1, 2)[i % 4], 4)
    cc = core if i < 4 else 1 - core
    return pl.multiple_of((zz * 2 + cc) * 128, 128)


def place_features(at, refs, dst):
    for i, ref in enumerate(refs):
        dst[:, pl.ds(feature_offset(at[2], at[3], i), 128)] = ref[...]


def spread(start, src, dst, sems):
    part = src.at[:, start : start + dst.shape[2]]
    copies = [pltpu.make_async_copy(part, dst.at[i], sems.at[i]) for i in range(dst.shape[0])]
    for copy in copies:
        copy.start()
    for copy in copies:
        copy.wait()


def pack(at, env, low, p0, p1, p2, p3):
    n = env.shape[0] // 4
    for d, out in enumerate((p0, p1, p2, p3)):
        for i, add in enumerate((d, d + 2)):
            src = pl.ds(pl.multiple_of(lax.rem(at[0] + add, 4) * n, n), n)
            out[i * n : (i + 1) * n, :] = env[src, :]
            out[(i + 2) * n : (i + 3) * n, :] = low[src, :]


def assemble(at, p0, p1, p2, p3, p4, p5, p6, p7, feats, low):
    n = low.shape[0]
    for i, ref in enumerate((p0, p1, p2, p3, p4, p5, p6, p7)):
        cols = pl.ds(feature_offset(at[2], at[3], i), 128)
        feats[:, cols] = ref[: 2 * n, :]
        low[:, cols] = ref[2 * n :, :]


def through_first(low, inv, high, rest):
    both = jnp.dot(low[...], inv[...], preferred_element_type=F32)
    high[...] = both.astype(BF16)
    rest[...] = (both - high[...].astype(F32)).astype(BF16)


def square(feats, qt, total):
    dots = jnp.dot(feats, qt, preferred_element_type=F32) * (1.0 / (total**0.5))
    return dots * dots


def kernel_slices(feats, qa, qb, k0, k1):
    n, start = k0.shape[0], 0
    for q in (qa, qb):
        cols = slice(start, start + q.shape[1])
        k = square(feats[...], q[...], q.shape[0])
        k0[:, cols] = k[:n].astype(BF16)
        k1[:, cols] = k[n:]
        start += q.shape[1]


def place_rows(at, refs, dst):
    color = lax.rem(at[0] + 2 * at[1], 4)
    for add, ref in zip((0, 1, 3, 2), refs):
        off = pl.multiple_of(lax.rem(color + add, 4) * ref.shape[0], ref.shape[0])
        dst[pl.ds(off, ref.shape[0]), :] = ref[...]


def right_side(at, a, b, c, d, high, rest, k1, t, rhs):
    place_rows(at, (a, b, c, d), rhs)
    low = jnp.dot(high[...], rhs[...], preferred_element_type=F32)
    low = low + jnp.dot(rest[...], rhs[...], preferred_element_type=F32)
    t[...] = (k1[...] - low).astype(BF16)


def first_solve(rhs, inv, s0):
    s0[...] = jnp.dot(inv[...], rhs[...], preferred_element_type=F32).astype(BF16)


def kernel_rows(at, qa, qb, p0, p1, p2, p3, p4, p5, p6, p7, out, feats):
    place_features(at, (p0, p1, p2, p3, p4, p5, p6, p7), feats)
    start = 0
    for q in (qa, qb):
        out[:, start : start + q.shape[1]] = square(feats[...], q[...], q.shape[0])
        start += q.shape[1]


def update(s0, low, k, out):
    out[...] = k[...] - jnp.dot(low[...], s0[...], preferred_element_type=F32)


def through_second(at, low, inv, out):
    here = at[0] + 4 * at[1]
    i, bm = pl.program_id(0), out.shape[0]
    solving = jnp.logical_and(here == 1, i < inv.shape[0] // bm)

    @pl.when(solving)
    def _():
        out[...] = inv[pl.ds(pl.multiple_of(lax.rem(i * bm, inv.shape[0]), bm), bm), :]

    @pl.when(jnp.logical_not(solving))
    def _():
        out[...] = jnp.dot(low[...], inv[...], preferred_element_type=F32).astype(BF16)


def last_step(at, a, b, c, d, s0, low, res, out, rhs):
    i = pl.program_id(0)
    here = at[0] + 4 * at[1]
    bm = out.shape[0]
    per_block = s0.shape[0] // bm

    @pl.when(i == 0)
    def _():
        place_rows(at, (a, b, c, d), rhs)

    first = i < per_block

    @pl.when(jnp.logical_and(first, here == 0))
    def _():
        out[...] = s0[pl.ds(pl.multiple_of(lax.rem(i, per_block) * bm, bm), bm), :]

    @pl.when(jnp.logical_and(first, here == 1))
    def _():
        out[...] = jnp.dot(low[...], rhs[...], preferred_element_type=F32).astype(BF16)

    @pl.when(jnp.logical_not(jnp.logical_and(first, here < 2)))
    def _():
        out[...] = (res[...] - jnp.dot(low[...], rhs[...], preferred_element_type=F32)).astype(BF16)


def per_device(lower_panel, sparse_desc, query_desc, diag_inv):
    blocks, width, _ = lower_panel.shape
    queries = query_desc.shape[0]
    here, part = lax.axis_index("rows"), lax.axis_index("pb")
    x, y = here % N, here // N
    z, core = part // 2, part % 2
    at = jnp.stack([x, y, z, core]).astype(jnp.int32)
    smem = pl.BlockSpec(memory_space=pltpu.SMEM)
    quarter = width // 4
    piece = sparse_desc.shape[2]
    feats = piece * 2 * N

    got = pl.pallas_call(
        pack,
        grid_spec=pltpu.PrefetchScalarGridSpec(
            num_scalar_prefetch=1,
            grid=(1,),
            in_specs=[
                pl.BlockSpec((None, width, piece), lambda i, at: (0, 0, 0)),
                pl.BlockSpec((None, width, piece), lambda i, at: (0, 0, at[2] * 2 + at[3])),
            ],
            out_specs=[pl.BlockSpec((width, piece), lambda i, at: (0, 0))] * 4,
        ),
        out_shape=[jax.ShapeDtypeStruct((width, piece), BF16)] * 4,
        compiler_params=params(56),
    )(at, sparse_desc, lower_panel)

    own_q = query_desc.T
    first_part = queries // 4

    def gather_queries(start, count, source):
        copies = pl.pallas_call(
            functools.partial(spread, start),
            in_specs=[whole()],
            out_specs=pl.BlockSpec(memory_space=pl.ANY),
            out_shape=jax.ShapeDtypeStruct((N * N, own_q.shape[0], count), BF16),
            scratch_shapes=[pltpu.SemaphoreType.DMA((N * N,))],
            compiler_params=params(56),
        )(source)
        return lax.all_to_all(copies, "rows", 0, 0, tiled=True).reshape(feats, count)

    qa = gather_queries(0, first_part, after(own_q, got[0]))

    own = sparse_desc.reshape(blocks * width, piece)
    early = after(own, got[0])
    envs = [own] + [lax.ppermute(early, "pb", z_perm(d)) for d in (1, -1)]

    got = [got[0]] + [
        lax.ppermute(got[d], "rows", [(0, d), (1, (1 + d) % N)]) for d in (1, 2, 3)
    ]
    from0 = pick(x, got)
    from1 = pick((x + 3) % N, got)
    n = quarter
    even = jnp.concatenate([from0[:n], from1[:n], from1[2 * n : 3 * n]])
    odd = jnp.concatenate([from0[n : 2 * n], from1[n : 2 * n], from1[3 * n :]])
    qb = gather_queries(first_part, queries - first_part, after(own_q, even))
    got_y = [even] + [
        lax.ppermute(even if d == 2 else odd, "rows", [(c, d * N + c) for c in range(N)])
        for d in (1, 2, 3)
    ]
    mine = pick(y, got_y)
    mine, _, _ = lax.optimization_barrier((mine, envs[1], envs[2]))
    slices = [mine] + [lax.ppermute(mine, "pb", z_perm(d)) for d in (1, -1, 2)]
    envs = envs + [lax.ppermute(after(own, slices[1]), "pb", z_perm(2))]
    slices = slices + [lax.ppermute(v, "pb", SWAP) for v in slices]

    unit = 2 * width * feats * queries
    def block(i):
        return pl.BlockSpec((None, width, width), lambda *_: (i, 0, 0))

    narrow = jax.ShapeDtypeStruct((quarter, width), BF16)
    slice_feats, low = pl.pallas_call(
        assemble,
        out_shape=(jax.ShapeDtypeStruct((2 * quarter, feats), BF16), narrow),
        in_specs=[smem] + [whole()] * 8,
        out_specs=(whole(),) * 2,
        compiler_params=params(16),
        cost_estimate=cost(6900000000, 22200000),
    )(at, *slices)
    high, rest = pl.pallas_call(
        through_first,
        grid=(1,),
        out_shape=(narrow, narrow),
        in_specs=[whole(), block(0)],
        out_specs=(whole(),) * 2,
        compiler_params=params(16),
        cost_estimate=cost(unit / 4, 5e6),
    )(low, diag_inv)
    second = pl.pallas_call(
        through_second,
        grid=(blocks * width // BM,),
        out_shape=jax.ShapeDtypeStruct((blocks * width, width), BF16),
        in_specs=[smem, pl.BlockSpec((BM, width), lambda i: (i, 1)), block(1)],
        out_specs=pl.BlockSpec((BM, width), lambda i: (i, 0)),
        compiler_params=params(20),
        cost_estimate=cost(unit / 50, 2e5),
    )(after(at, high), lower_panel.reshape(blocks * width, 2 * width), diag_inv)
    k0, k1 = pl.pallas_call(
        kernel_slices,
        out_shape=(
            jax.ShapeDtypeStruct((quarter, queries), BF16),
            jax.ShapeDtypeStruct((quarter, queries), F32),
        ),
        in_specs=[whole()] * 3,
        out_specs=(whole(), whole()),
        compiler_params=params(16),
        cost_estimate=cost(unit / 2, 5e6),
    )(after(slice_feats, high, second), qa, qb)

    def neighbours(v):
        return (
            v,
            lax.ppermute(v, "rows", x_perm(-1)),
            lax.ppermute(v, "rows", x_perm(1)),
            lax.ppermute(v, "rows", y_perm(-1)),
        )

    ready = [after(e, slice_feats) for e in envs[:3]] + [after(envs[3], k0)]
    envs = envs + [lax.ppermute(v, "pb", SWAP) for v in ready]

    bm = BM
    rows = blocks * width
    panel = lower_panel.reshape(rows, 2 * width)
    k_rows = pl.pallas_call(
        kernel_rows,
        grid=(rows // bm,),
        out_shape=jax.ShapeDtypeStruct((rows, queries), F32),
        in_specs=[smem, whole(), whole()] + [pl.BlockSpec((bm, piece), lambda i: (i, 0))] * 8,
        out_specs=pl.BlockSpec((bm, queries), lambda i: (i, 0)),
        scratch_shapes=[pltpu.VMEM((bm, feats), BF16)],
        compiler_params=params(16),
        cost_estimate=cost(unit * 2, 14e6),
    )(at, qa, qb, *envs)
    t, rhs = pl.pallas_call(
        right_side,
        out_shape=(
            jax.ShapeDtypeStruct((quarter, queries), BF16),
            jax.ShapeDtypeStruct((width, queries), BF16),
        ),
        in_specs=[smem] + [whole()] * 7,
        out_specs=(whole(),) * 2,
        compiler_params=params(20),
        cost_estimate=cost(unit * 0.5, 8e6),
    )(at, *neighbours(k0), high, rest, after(k1, k_rows))
    s0 = pl.pallas_call(
        first_solve,
        grid=(1,),
        out_shape=jax.ShapeDtypeStruct((width, queries), BF16),
        in_specs=[whole(), block(0)],
        out_specs=whole(),
        compiler_params=params(20),
        cost_estimate=cost(unit, 6e6),
    )(rhs, diag_inv)

    res = pl.pallas_call(
        update,
        grid=(rows // bm,),
        out_shape=jax.ShapeDtypeStruct((rows, queries), F32),
        in_specs=[
            whole(),
            pl.BlockSpec((bm, width), lambda i: (i, 0)),
            pl.BlockSpec((bm, queries), lambda i: (i, 0)),
        ],
        out_specs=pl.BlockSpec((bm, queries), lambda i: (i, 0)),
        input_output_aliases={2: 0},
        compiler_params=params(16),
        cost_estimate=cost(unit * 2, 22e6),
    )(s0, panel, k_rows)

    out = pl.pallas_call(
        last_step,
        grid=(rows // bm,),
        out_shape=jax.ShapeDtypeStruct((rows, queries), BF16),
        in_specs=[smem]
        + [whole()] * 4
        + [
            whole(),
            pl.BlockSpec((bm, width), lambda i: (i, 0)),
            pl.BlockSpec((bm, queries), lambda i: (i, 0)),
        ],
        out_specs=pl.BlockSpec((bm, queries), lambda i: (i, 0)),
        scratch_shapes=[pltpu.VMEM((width, queries), BF16)],
        compiler_params=params(20),
        cost_estimate=cost(unit * 2, 18e6),
    )(at, *neighbours(t), s0, second, res)
    return out.reshape(blocks, width, queries)


def solution(mesh):
    return jax.shard_map(
        per_device,
        mesh=mesh,
        in_specs=(P(None, "rows", None), P(None, "rows", "pb"), P("pb", "rows"), P()),
        out_specs=P(None, "rows", "pb"),
        check_vma=False,
    )
```

```python
import functools

import jax
import jax.numpy as jnp
from jax import lax
from jax.experimental import pallas as pl
from jax.experimental.pallas import tpu as pltpu
from jax.sharding import PartitionSpec as P

BF16, F32 = jnp.bfloat16, jnp.float32
N = 4
BM = 512


def x_perm(d):
    return [(r, (r // N) * N + (r % N + d) % N) for r in range(N * N)]


def y_perm(d):
    return [(r, ((r // N + d) % N) * N + r % N) for r in range(N * N)]


def z_perm(d):
    return [(p, ((p // 2 + d) % N) * 2 + p % 2) for p in range(2 * N)]


SWAP = [(p, p ^ 1) for p in range(2 * N)]


def pick(index, choices):
    out = choices[0]
    for i in range(1, len(choices)):
        out = jnp.where(index == i, choices[i], out)
    return out


def after(value, *others):
    return lax.optimization_barrier((value,) + others)[0]


def params(mib):
    return pltpu.CompilerParams(vmem_limit_bytes=mib * 1024 * 1024)


def cost(flops, moved):
    return pl.CostEstimate(flops=int(flops), bytes_accessed=int(moved), transcendentals=0)


def whole():
    return pl.BlockSpec(memory_space=pltpu.VMEM)


def feature_offset(z, core, i):
    zz = lax.rem(z + (0, 3, 1, 2)[i % 4], 4)
    cc = core if i < 4 else 1 - core
    return pl.multiple_of((zz * 2 + cc) * 128, 128)


def place_features(at, refs, dst):
    for i, ref in enumerate(refs):
        dst[:, pl.ds(feature_offset(at[2], at[3], i), 128)] = ref[...]


def spread(start, src, dst, sems):
    part = src.at[:, start : start + dst.shape[2]]
    copies = [pltpu.make_async_copy(part, dst.at[i], sems.at[i]) for i in range(dst.shape[0])]
    for copy in copies:
        copy.start()
    for copy in copies:
        copy.wait()


def pack(at, env, low, p0, p1, p2, p3):
    n = env.shape[0] // 4
    for d, out in enumerate((p0, p1, p2, p3)):
        for i, add in enumerate((d, d + 2)):
            src = pl.ds(pl.multiple_of(lax.rem(at[0] + add, 4) * n, n), n)
            out[i * n : (i + 1) * n, :] = env[src, :]
            out[(i + 2) * n : (i + 3) * n, :] = low[src, :]


def assemble(at, p0, p1, p2, p3, p4, p5, p6, p7, feats, low):
    n = low.shape[0]
    for i, ref in enumerate((p0, p1, p2, p3, p4, p5, p6, p7)):
        cols = pl.ds(feature_offset(at[2], at[3], i), 128)
        feats[:, cols] = ref[: 2 * n, :]
        low[:, cols] = ref[2 * n :, :]


def through_first(low, inv, high, rest):
    both = jnp.dot(low[...], inv[...], preferred_element_type=F32)
    high[...] = both.astype(BF16)
    rest[...] = (both - high[...].astype(F32)).astype(BF16)


def square(feats, qt, total):
    dots = jnp.dot(feats, qt, preferred_element_type=F32) * (1.0 / (total**0.5))
    return dots * dots


def kernel_slices(feats_hbm, qa_hbm, qb, k0, k1, feats, qa, sems):
    copies = [
        pltpu.make_async_copy(feats_hbm, feats, sems.at[0]),
        pltpu.make_async_copy(qa_hbm, qa, sems.at[1]),
    ]
    for copy in copies:
        copy.start()
    for copy in copies:
        copy.wait()
    n, start = k0.shape[0], 0
    for q in (qa, qb):
        cols = slice(start, start + q.shape[1])
        k = square(feats[...], q[...], q.shape[0])
        k0[:, cols] = k[:n].astype(BF16)
        k1[:, cols] = k[n:]
        start += q.shape[1]


def place_rows(at, refs, dst):
    color = lax.rem(at[0] + 2 * at[1], 4)
    for add, ref in zip((0, 1, 3, 2), refs):
        off = pl.multiple_of(lax.rem(color + add, 4) * ref.shape[0], ref.shape[0])
        dst[pl.ds(off, ref.shape[0]), :] = ref[...]


def right_side(at, a, b, c, d, high, rest, k1, t, rhs):
    place_rows(at, (a, b, c, d), rhs)
    low = jnp.dot(high[...], rhs[...], preferred_element_type=F32)
    low = low + jnp.dot(rest[...], rhs[...], preferred_element_type=F32)
    t[...] = (k1[...] - low).astype(BF16)


def first_solve(rhs, inv, s0):
    s0[...] = jnp.dot(inv[...], rhs[...], preferred_element_type=F32).astype(BF16)


def kernel_rows(at, qa, qb, p0, p1, p2, p3, p4, p5, p6, p7, out, feats):
    place_features(at, (p0, p1, p2, p3, p4, p5, p6, p7), feats)
    start = 0
    for q in (qa, qb):
        out[:, start : start + q.shape[1]] = square(feats[...], q[...], q.shape[0])
        start += q.shape[1]


def update(s0, low, k, out):
    out[...] = k[...] - jnp.dot(low[...], s0[...], preferred_element_type=F32)


def through_second(at, low, inv, out):
    here = at[0] + 4 * at[1]
    i, bm = pl.program_id(0), out.shape[0]
    solving = jnp.logical_and(here == 1, i < inv.shape[0] // bm)

    @pl.when(solving)
    def _():
        out[...] = inv[pl.ds(pl.multiple_of(lax.rem(i * bm, inv.shape[0]), bm), bm), :]

    @pl.when(jnp.logical_not(solving))
    def _():
        out[...] = jnp.dot(low[...], inv[...], preferred_element_type=F32).astype(BF16)


def last_step(at, a, b, c, d, s0, low, res, out, rhs):
    i = pl.program_id(0)
    here = at[0] + 4 * at[1]
    bm = out.shape[0]
    per_block = s0.shape[0] // bm

    @pl.when(i == 0)
    def _():
        place_rows(at, (a, b, c, d), rhs)

    first = i < per_block

    @pl.when(jnp.logical_and(first, here == 0))
    def _():
        out[...] = s0[pl.ds(pl.multiple_of(lax.rem(i, per_block) * bm, bm), bm), :]

    @pl.when(jnp.logical_and(first, here == 1))
    def _():
        out[...] = jnp.dot(low[...], rhs[...], preferred_element_type=F32).astype(BF16)

    @pl.when(jnp.logical_not(jnp.logical_and(first, here < 2)))
    def _():
        out[...] = (res[...] - jnp.dot(low[...], rhs[...], preferred_element_type=F32)).astype(BF16)


def per_device(lower_panel, sparse_desc, query_desc, diag_inv):
    blocks, width, _ = lower_panel.shape
    queries = query_desc.shape[0]
    here, part = lax.axis_index("rows"), lax.axis_index("pb")
    x, y = here % N, here // N
    z, core = part // 2, part % 2
    at = jnp.stack([x, y, z, core]).astype(jnp.int32)
    smem = pl.BlockSpec(memory_space=pltpu.SMEM)
    quarter = width // 4
    piece = sparse_desc.shape[2]
    feats = piece * 2 * N

    got = pl.pallas_call(
        pack,
        grid_spec=pltpu.PrefetchScalarGridSpec(
            num_scalar_prefetch=1,
            grid=(1,),
            in_specs=[
                pl.BlockSpec((None, width, piece), lambda i, at: (0, 0, 0)),
                pl.BlockSpec((None, width, piece), lambda i, at: (0, 0, at[2] * 2 + at[3])),
            ],
            out_specs=[pl.BlockSpec((width, piece), lambda i, at: (0, 0))] * 4,
        ),
        out_shape=[jax.ShapeDtypeStruct((width, piece), BF16)] * 4,
        compiler_params=params(56),
    )(at, sparse_desc, lower_panel)

    own_q = query_desc.T
    first_part = queries // 4

    def gather_queries(start, count, source):
        copies = pl.pallas_call(
            functools.partial(spread, start),
            in_specs=[whole()],
            out_specs=pl.BlockSpec(memory_space=pl.ANY),
            out_shape=jax.ShapeDtypeStruct((N * N, own_q.shape[0], count), BF16),
            scratch_shapes=[pltpu.SemaphoreType.DMA((N * N,))],
            compiler_params=params(56),
        )(source)
        return lax.all_to_all(copies, "rows", 0, 0, tiled=True).reshape(feats, count)

    qa = gather_queries(0, first_part, after(own_q, got[0]))

    own = sparse_desc.reshape(blocks * width, piece)
    early = after(own, got[0])
    envs = [own] + [lax.ppermute(early, "pb", z_perm(d)) for d in (1, -1)]

    got = [got[0]] + [
        lax.ppermute(got[d], "rows", [(0, d), (1, (1 + d) % N)]) for d in (1, 2, 3)
    ]
    from0 = pick(x, got)
    from1 = pick((x + 3) % N, got)
    n = quarter
    even = jnp.concatenate([from0[:n], from1[:n], from1[2 * n : 3 * n]])
    odd = jnp.concatenate([from0[n : 2 * n], from1[n : 2 * n], from1[3 * n :]])
    qb = gather_queries(first_part, queries - first_part, after(own_q, even))
    got_y = [even] + [
        lax.ppermute(even if d == 2 else odd, "rows", [(c, d * N + c) for c in range(N)])
        for d in (1, 2, 3)
    ]
    mine = pick(y, got_y)
    mine, _, _ = lax.optimization_barrier((mine, envs[1], envs[2]))
    slices = [mine] + [lax.ppermute(mine, "pb", z_perm(d)) for d in (1, -1, 2)]
    envs = envs + [lax.ppermute(after(own, slices[1]), "pb", z_perm(2))]
    slices = slices + [lax.ppermute(v, "pb", SWAP) for v in slices]

    unit = 2 * width * feats * queries
    def block(i):
        return pl.BlockSpec((None, width, width), lambda *_: (i, 0, 0))

    narrow = jax.ShapeDtypeStruct((quarter, width), BF16)
    slice_feats, low = pl.pallas_call(
        assemble,
        out_shape=(pltpu.HBM((2 * quarter, feats), BF16), narrow),
        in_specs=[smem] + [whole()] * 8,
        out_specs=(whole(),) * 2,
        compiler_params=params(16),
        cost_estimate=cost(6900000000, 22200000),
    )(at, *slices)
    high, rest = pl.pallas_call(
        through_first,
        grid=(1,),
        out_shape=(narrow, narrow),
        in_specs=[whole(), block(0)],
        out_specs=(whole(),) * 2,
        compiler_params=params(16),
        cost_estimate=cost(unit / 4, 5e6),
    )(low, diag_inv)
    second = pl.pallas_call(
        through_second,
        grid=(blocks * width // BM,),
        out_shape=pltpu.HBM((blocks * width, width), BF16),
        in_specs=[smem, pl.BlockSpec((BM, width), lambda i: (i, 1)), block(1)],
        out_specs=pl.BlockSpec((BM, width), lambda i: (i, 0)),
        compiler_params=params(20),
        cost_estimate=cost(unit / 50, 2e5),
    )(after(at, high), lower_panel.reshape(blocks * width, 2 * width), diag_inv)
    k0, k1 = pl.pallas_call(
        kernel_slices,
        out_shape=(
            jax.ShapeDtypeStruct((quarter, queries), BF16),
            jax.ShapeDtypeStruct((quarter, queries), F32),
        ),
        in_specs=[pl.BlockSpec(memory_space=pltpu.HBM)] * 2 + [whole()],
        out_specs=(whole(), whole()),
        scratch_shapes=[
            pltpu.VMEM((2 * quarter, feats), BF16),
            pltpu.VMEM((feats, first_part), BF16),
            pltpu.SemaphoreType.DMA((2,)),
        ],
        compiler_params=params(16),
        cost_estimate=cost(unit / 2, 5e6),
    )(after(slice_feats, high, second), qa, qb)

    def neighbours(v):
        return (
            v,
            lax.ppermute(v, "rows", x_perm(-1)),
            lax.ppermute(v, "rows", x_perm(1)),
            lax.ppermute(v, "rows", y_perm(-1)),
        )

    ready = [after(e, slice_feats) for e in envs[:3]] + [after(envs[3], k0)]
    envs = envs + [lax.ppermute(v, "pb", SWAP) for v in ready]

    bm = BM
    rows = blocks * width
    panel = lower_panel.reshape(rows, 2 * width)
    k_rows = pl.pallas_call(
        kernel_rows,
        grid=(rows // bm,),
        out_shape=jax.ShapeDtypeStruct((rows, queries), F32),
        in_specs=[smem, whole(), whole()] + [pl.BlockSpec((bm, piece), lambda i: (i, 0))] * 8,
        out_specs=pl.BlockSpec((bm, queries), lambda i: (i, 0)),
        scratch_shapes=[pltpu.VMEM((bm, feats), BF16)],
        compiler_params=params(16),
        cost_estimate=cost(unit * 2, 14e6),
    )(at, qa, qb, *envs)
    t, rhs = pl.pallas_call(
        right_side,
        out_shape=(
            jax.ShapeDtypeStruct((quarter, queries), BF16),
            jax.ShapeDtypeStruct((width, queries), BF16),
        ),
        in_specs=[smem] + [whole()] * 7,
        out_specs=(whole(),) * 2,
        compiler_params=params(20),
        cost_estimate=cost(unit * 0.5, 8e6),
    )(at, *neighbours(k0), high, rest, after(k1, k_rows))
    s0 = pl.pallas_call(
        first_solve,
        grid=(1,),
        out_shape=jax.ShapeDtypeStruct((width, queries), BF16),
        in_specs=[whole(), block(0)],
        out_specs=whole(),
        compiler_params=params(20),
        cost_estimate=cost(unit, 6e6),
    )(rhs, diag_inv)

    res = pl.pallas_call(
        update,
        grid=(rows // bm,),
        out_shape=jax.ShapeDtypeStruct((rows, queries), F32),
        in_specs=[
            whole(),
            pl.BlockSpec((bm, width), lambda i: (i, 0)),
            pl.BlockSpec((bm, queries), lambda i: (i, 0)),
        ],
        out_specs=pl.BlockSpec((bm, queries), lambda i: (i, 0)),
        input_output_aliases={2: 0},
        compiler_params=params(16),
        cost_estimate=cost(unit * 2, 22e6),
    )(s0, panel, k_rows)

    out = pl.pallas_call(
        last_step,
        grid=(rows // bm,),
        out_shape=jax.ShapeDtypeStruct((rows, queries), BF16),
        in_specs=[smem]
        + [whole()] * 4
        + [
            whole(),
            pl.BlockSpec((bm, width), lambda i: (i, 0)),
            pl.BlockSpec((bm, queries), lambda i: (i, 0)),
        ],
        out_specs=pl.BlockSpec((bm, queries), lambda i: (i, 0)),
        scratch_shapes=[pltpu.VMEM((width, queries), BF16)],
        compiler_params=params(20),
        cost_estimate=cost(unit * 2, 18e6),
    )(at, *neighbours(t), s0, second, res)
    return out.reshape(blocks, width, queries)


def solution(mesh):
    return jax.shard_map(
        per_device,
        mesh=mesh,
        in_specs=(P(None, "rows", None), P(None, "rows", "pb"), P("pb", "rows"), P()),
        out_specs=P(None, "rows", "pb"),
        check_vma=False,
    )
```

```python
import functools

import jax
import jax.numpy as jnp
from jax import lax
from jax.experimental import pallas as pl
from jax.experimental.pallas import tpu as pltpu
from jax.sharding import PartitionSpec as P

BF16, F32 = jnp.bfloat16, jnp.float32
N = 4
BM = 512


def x_perm(d):
    return [(r, (r // N) * N + (r % N + d) % N) for r in range(N * N)]


def y_perm(d):
    return [(r, ((r // N + d) % N) * N + r % N) for r in range(N * N)]


def z_perm(d):
    return [(p, ((p // 2 + d) % N) * 2 + p % 2) for p in range(2 * N)]


SWAP = [(p, p ^ 1) for p in range(2 * N)]


def pick(index, choices):
    out = choices[0]
    for i in range(1, len(choices)):
        out = jnp.where(index == i, choices[i], out)
    return out


def after(value, *others):
    return lax.optimization_barrier((value,) + others)[0]


def params(mib):
    return pltpu.CompilerParams(vmem_limit_bytes=mib * 1024 * 1024)


def cost(flops, moved):
    return pl.CostEstimate(flops=int(flops), bytes_accessed=int(moved), transcendentals=0)


def whole():
    return pl.BlockSpec(memory_space=pltpu.VMEM)


def feature_offset(z, core, i):
    zz = lax.rem(z + (0, 3, 1, 2)[i % 4], 4)
    cc = core if i < 4 else 1 - core
    return pl.multiple_of((zz * 2 + cc) * 128, 128)


def place_features(at, refs, dst):
    for i, ref in enumerate(refs):
        dst[:, pl.ds(feature_offset(at[2], at[3], i), 128)] = ref[...]


def spread(start, src, dst, sems):
    part = src.at[:, start : start + dst.shape[2]]
    copies = [pltpu.make_async_copy(part, dst.at[i], sems.at[i]) for i in range(dst.shape[0])]
    for copy in copies:
        copy.start()
    for copy in copies:
        copy.wait()


def pack(at, env, low, p0, p1, p2, p3):
    n = env.shape[0] // 4
    for d, out in enumerate((p0, p1, p2, p3)):
        for i, add in enumerate((d, d + 2)):
            src = pl.ds(pl.multiple_of(lax.rem(at[0] + add, 4) * n, n), n)
            out[i * n : (i + 1) * n, :] = env[src, :]
            out[(i + 2) * n : (i + 3) * n, :] = low[src, :]


def assemble(at, p0, p1, p2, p3, p4, p5, p6, p7, feats, low):
    n = low.shape[0]
    for i, ref in enumerate((p0, p1, p2, p3, p4, p5, p6, p7)):
        cols = pl.ds(feature_offset(at[2], at[3], i), 128)
        feats[:, cols] = ref[: 2 * n, :]
        low[:, cols] = ref[2 * n :, :]


def through_first(low, inv, high, rest):
    both = jnp.dot(low[...], inv[...], preferred_element_type=F32)
    high[...] = both.astype(BF16)
    rest[...] = (both - high[...].astype(F32)).astype(BF16)


def square(feats, qt, total):
    dots = jnp.dot(feats, qt, preferred_element_type=F32) * (1.0 / (total**0.5))
    return dots * dots


def kernel_slices(feats, qa, qb, k0, k1):
    n, start = k0.shape[0], 0
    for q in (qa, qb):
        cols = slice(start, start + q.shape[1])
        k = square(feats[...], q[...], q.shape[0])
        k0[:, cols] = k[:n].astype(BF16)
        k1[:, cols] = k[n:]
        start += q.shape[1]


def place_rows(at, refs, dst):
    color = lax.rem(at[0] + 2 * at[1], 4)
    for add, ref in zip((0, 1, 3, 2), refs):
        off = pl.multiple_of(lax.rem(color + add, 4) * ref.shape[0], ref.shape[0])
        dst[pl.ds(off, ref.shape[0]), :] = ref[...]


def right_side(at, a, b, c, d, high, rest, k1, t, rhs):
    place_rows(at, (a, b, c, d), rhs)
    low = jnp.dot(high[...], rhs[...], preferred_element_type=F32)
    low = low + jnp.dot(rest[...], rhs[...], preferred_element_type=F32)
    t[...] = (k1[...] - low).astype(BF16)


def first_solve(rhs, inv, s0):
    s0[...] = jnp.dot(inv[...], rhs[...], preferred_element_type=F32).astype(BF16)


def kernel_rows(at, qa, qb, p0, p1, p2, p3, p4, p5, p6, p7, out, feats):
    place_features(at, (p0, p1, p2, p3, p4, p5, p6, p7), feats)
    start = 0
    for q in (qa, qb):
        out[:, start : start + q.shape[1]] = square(feats[...], q[...], q.shape[0])
        start += q.shape[1]


def update(s0, low, k, out):
    out[...] = k[...] - jnp.dot(low[...], s0[...], preferred_element_type=F32)


def through_second(at, low, inv, out):
    here = at[0] + 4 * at[1]
    i, bm = pl.program_id(0), out.shape[0]
    solving = jnp.logical_and(here == 1, i < inv.shape[0] // bm)

    @pl.when(solving)
    def _():
        out[...] = inv[pl.ds(pl.multiple_of(lax.rem(i * bm, inv.shape[0]), bm), bm), :]

    @pl.when(jnp.logical_not(solving))
    def _():
        out[...] = jnp.dot(low[...], inv[...], preferred_element_type=F32).astype(BF16)


def last_step(at, a, b, c, d, s0, low, res, out, rhs):
    i = pl.program_id(0)
    here = at[0] + 4 * at[1]
    bm = out.shape[0]
    per_block = s0.shape[0] // bm

    @pl.when(i == 0)
    def _():
        place_rows(at, (a, b, c, d), rhs)

    first = i < per_block

    @pl.when(jnp.logical_and(first, here == 0))
    def _():
        out[...] = s0[pl.ds(pl.multiple_of(lax.rem(i, per_block) * bm, bm), bm), :]

    @pl.when(jnp.logical_and(first, here == 1))
    def _():
        out[...] = jnp.dot(low[...], rhs[...], preferred_element_type=F32).astype(BF16)

    @pl.when(jnp.logical_not(jnp.logical_and(first, here < 2)))
    def _():
        out[...] = (res[...] - jnp.dot(low[...], rhs[...], preferred_element_type=F32)).astype(BF16)


def per_device(lower_panel, sparse_desc, query_desc, diag_inv):
    blocks, width, _ = lower_panel.shape
    queries = query_desc.shape[0]
    here, part = lax.axis_index("rows"), lax.axis_index("pb")
    x, y = here % N, here // N
    z, core = part // 2, part % 2
    at = jnp.stack([x, y, z, core]).astype(jnp.int32)
    smem = pl.BlockSpec(memory_space=pltpu.SMEM)
    quarter = width // 4
    piece = sparse_desc.shape[2]
    feats = piece * 2 * N

    got = pl.pallas_call(
        pack,
        grid_spec=pltpu.PrefetchScalarGridSpec(
            num_scalar_prefetch=1,
            grid=(1,),
            in_specs=[
                pl.BlockSpec((None, width, piece), lambda i, at: (0, 0, 0)),
                pl.BlockSpec((None, width, piece), lambda i, at: (0, 0, at[2] * 2 + at[3])),
            ],
            out_specs=[pl.BlockSpec((width, piece), lambda i, at: (0, 0))] * 4,
        ),
        out_shape=[jax.ShapeDtypeStruct((width, piece), BF16)] * 4,
        compiler_params=params(56),
    )(at, sparse_desc, lower_panel)

    own_q = query_desc.T
    first_part = queries // 8

    def gather_queries(start, count, source):
        copies = pl.pallas_call(
            functools.partial(spread, start),
            in_specs=[whole()],
            out_specs=pl.BlockSpec(memory_space=pl.ANY),
            out_shape=jax.ShapeDtypeStruct((N * N, own_q.shape[0], count), BF16),
            scratch_shapes=[pltpu.SemaphoreType.DMA((N * N,))],
            compiler_params=params(56),
        )(source)
        return lax.all_to_all(copies, "rows", 0, 0, tiled=True).reshape(feats, count)

    qa = gather_queries(0, first_part, after(own_q, got[0]))

    own = sparse_desc.reshape(blocks * width, piece)
    early = after(own, got[0])
    envs = [own] + [lax.ppermute(early, "pb", z_perm(d)) for d in (1, -1)]

    got = [got[0]] + [
        lax.ppermute(got[d], "rows", [(0, d), (1, (1 + d) % N)]) for d in (1, 2, 3)
    ]
    from0 = pick(x, got)
    from1 = pick((x + 3) % N, got)
    n = quarter
    even = jnp.concatenate([from0[:n], from1[:n], from1[2 * n : 3 * n]])
    odd = jnp.concatenate([from0[n : 2 * n], from1[n : 2 * n], from1[3 * n :]])
    qb = gather_queries(first_part, queries - first_part, after(own_q, even))
    got_y = [even] + [
        lax.ppermute(even if d == 2 else odd, "rows", [(c, d * N + c) for c in range(N)])
        for d in (1, 2, 3)
    ]
    mine = pick(y, got_y)
    mine, _, _ = lax.optimization_barrier((mine, envs[1], envs[2]))
    slices = [mine] + [lax.ppermute(mine, "pb", z_perm(d)) for d in (1, -1, 2)]
    envs = envs + [lax.ppermute(after(own, slices[1]), "pb", z_perm(2))]
    slices = slices + [lax.ppermute(v, "pb", SWAP) for v in slices]

    unit = 2 * width * feats * queries
    def block(i):
        return pl.BlockSpec((None, width, width), lambda *_: (i, 0, 0))

    narrow = jax.ShapeDtypeStruct((quarter, width), BF16)
    slice_feats, low = pl.pallas_call(
        assemble,
        out_shape=(jax.ShapeDtypeStruct((2 * quarter, feats), BF16), narrow),
        in_specs=[smem] + [whole()] * 8,
        out_specs=(whole(),) * 2,
        compiler_params=params(16),
        cost_estimate=cost(9200000000, 29600000),
    )(at, *slices)
    high, rest = pl.pallas_call(
        through_first,
        grid=(1,),
        out_shape=(narrow, narrow),
        in_specs=[whole(), block(0)],
        out_specs=(whole(),) * 2,
        compiler_params=params(16),
        cost_estimate=cost(unit / 4, 5e6),
    )(low, diag_inv)
    second = pl.pallas_call(
        through_second,
        grid=(blocks * width // BM,),
        out_shape=jax.ShapeDtypeStruct((blocks * width, width), BF16),
        in_specs=[smem, pl.BlockSpec((BM, width), lambda i: (i, 1)), block(1)],
        out_specs=pl.BlockSpec((BM, width), lambda i: (i, 0)),
        compiler_params=params(20),
        cost_estimate=cost(unit / 50, 2e5),
    )(after(at, high), lower_panel.reshape(blocks * width, 2 * width), diag_inv)
    k0, k1 = pl.pallas_call(
        kernel_slices,
        out_shape=(
            jax.ShapeDtypeStruct((quarter, queries), BF16),
            jax.ShapeDtypeStruct((quarter, queries), F32),
        ),
        in_specs=[whole()] * 3,
        out_specs=(whole(), whole()),
        compiler_params=params(16),
        cost_estimate=cost(unit / 2, 5e6),
    )(after(slice_feats, high, second), qa, qb)

    def neighbours(v):
        return (
            v,
            lax.ppermute(v, "rows", x_perm(-1)),
            lax.ppermute(v, "rows", x_perm(1)),
            lax.ppermute(v, "rows", y_perm(-1)),
        )

    ready = [after(e, slice_feats) for e in envs[:3]] + [after(envs[3], k0)]
    envs = envs + [lax.ppermute(v, "pb", SWAP) for v in ready]

    bm = BM
    rows = blocks * width
    panel = lower_panel.reshape(rows, 2 * width)
    k_rows = pl.pallas_call(
        kernel_rows,
        grid=(rows // bm,),
        out_shape=jax.ShapeDtypeStruct((rows, queries), F32),
        in_specs=[smem, whole(), whole()] + [pl.BlockSpec((bm, piece), lambda i: (i, 0))] * 8,
        out_specs=pl.BlockSpec((bm, queries), lambda i: (i, 0)),
        scratch_shapes=[pltpu.VMEM((bm, feats), BF16)],
        compiler_params=params(16),
        cost_estimate=cost(unit * 2, 14e6),
    )(at, qa, qb, *envs)
    t, rhs = pl.pallas_call(
        right_side,
        out_shape=(
            jax.ShapeDtypeStruct((quarter, queries), BF16),
            jax.ShapeDtypeStruct((width, queries), BF16),
        ),
        in_specs=[smem] + [whole()] * 7,
        out_specs=(whole(),) * 2,
        compiler_params=params(20),
        cost_estimate=cost(unit * 0.5, 8e6),
    )(at, *neighbours(k0), high, rest, after(k1, k_rows))
    s0 = pl.pallas_call(
        first_solve,
        grid=(1,),
        out_shape=jax.ShapeDtypeStruct((width, queries), BF16),
        in_specs=[whole(), block(0)],
        out_specs=whole(),
        compiler_params=params(20),
        cost_estimate=cost(unit, 6e6),
    )(rhs, diag_inv)

    res = pl.pallas_call(
        update,
        grid=(rows // bm,),
        out_shape=jax.ShapeDtypeStruct((rows, queries), F32),
        in_specs=[
            whole(),
            pl.BlockSpec((bm, width), lambda i: (i, 0)),
            pl.BlockSpec((bm, queries), lambda i: (i, 0)),
        ],
        out_specs=pl.BlockSpec((bm, queries), lambda i: (i, 0)),
        input_output_aliases={2: 0},
        compiler_params=params(16),
        cost_estimate=cost(unit * 2, 22e6),
    )(s0, panel, k_rows)

    out = pl.pallas_call(
        last_step,
        grid=(rows // bm,),
        out_shape=jax.ShapeDtypeStruct((rows, queries), BF16),
        in_specs=[smem]
        + [whole()] * 4
        + [
            whole(),
            pl.BlockSpec((bm, width), lambda i: (i, 0)),
            pl.BlockSpec((bm, queries), lambda i: (i, 0)),
        ],
        out_specs=pl.BlockSpec((bm, queries), lambda i: (i, 0)),
        scratch_shapes=[pltpu.VMEM((width, queries), BF16)],
        compiler_params=params(20),
        cost_estimate=cost(unit * 2, 18e6),
    )(at, *neighbours(t), s0, second, res)
    return out.reshape(blocks, width, queries)


def solution(mesh):
    return jax.shard_map(
        per_device,
        mesh=mesh,
        in_specs=(P(None, "rows", None), P(None, "rows", "pb"), P("pb", "rows"), P()),
        out_specs=P(None, "rows", "pb"),
        check_vma=False,
    )
```
